256 devices in a mesh: dp: 128 (over x, y_hi, z, core), head: 2 (over y_lo).
Axes of the slice: x: 4, y: 4 (y_hi: 2, y_lo: 2; y = y_hi * 2 + y_lo), z: 8, core: 2. Of those that a mesh axis runs over, the one named last changes fastest.
Arguments:
- picture_tower_summary: bfloat16 [16384, 1536], P('dp'), may hold values from -24 to 24
- caption_tower_summary: bfloat16 [16384, 1536], P('dp'), may hold values from -24 to 24
- picture_head_matrix: bfloat16 [1536, 1536], P(None, 'head'), may hold values from -0.00390625 to 0.00390625
- caption_head_matrix: bfloat16 [1536, 1536], P(None, 'head'), may hold values from -0.00390625 to 0.00390625
- matching_caption_row: int32 [128, 128], P('dp'), may hold values from 0 to 127, each once within a row
- affinity_scale: float32 [1], replicated, may hold values from 4 to 16
- affinity_offset: float32 [1], replicated, may hold values from -4 to -2
Outputs:
- image_loss: float32 [16384], P('dp')
- image_grad_w: float32 [1536, 1536], P('dp', 'head')
- text_grad_w: float32 [1536, 1536], P('dp', 'head')
The draws below stay inside these ranges and needn't reach their ends.
Inputs may be any that keep to these rules, and one draw needn't show every extreme that they name: Each row of matching_caption_row is a permutation of 0..127.
All inputs are finite; a program needn't handle non-finite values.
Results may differ from the reference program's by a relative error of at most 0.0045.
Values may be sent and summed in bfloat16 or wider, within the bound.
A program may use at most 128 MiB of HBM per device.

```python
import math
import jax
import jax.numpy as jnp
from jax import lax

WIDTH = 1536
EMBED = 1536
ROWS = 128
REACH = 4
BLOCKS = 128
TOKENS = 16384


def raised(array, own_key, source, target, parts, factor):
    def block_of(position):
        return (jnp.arange(array.shape[position]) // (array.shape[position] // parts)).reshape((-1,) + (1,) * (array.ndim - 1 - position))

    one_side = jax.random.permutation(own_key, parts)[block_of(target)]
    second = (block_of(target) + parts // 2) % parts
    return jnp.where((block_of(source) == one_side) | (block_of(source) == second), factor * array, array)


def shard_levels(key, shape, shards, least, top_value):
    level, own = 1.0, jax.random.fold_in(key, 6)
    for axis_at, parts in shards:
        steps = jnp.exp(jax.random.uniform(jax.random.fold_in(own, axis_at), (parts,), jnp.float32, least / len(shards), top_value / len(shards)))
        level = level * jnp.repeat(steps, shape[axis_at] // parts).reshape([-1 if axis == axis_at else 1 for axis in range(len(shape))])
    return level


def scatter_about(own_key, extent, spread, reach, split=(), kind=jnp.bfloat16):
    loudness = shard_levels(own_key, extent, split, -0.22, 0.18) if split else 1.0
    result = jax.random.normal(own_key, extent, jnp.float32) * spread * loudness
    return jnp.minimum(jnp.maximum(result, -reach), reach).astype(kind)


def heavy_noise(stream_key, shape, deviation, bound, cuts, heavy, kind=jnp.bfloat16):
    values = deviation * jax.random.normal(stream_key, shape, jnp.float32)
    if cuts:
        values = values * shard_levels(stream_key, shape, cuts, -0.22, 0.18)
    return jnp.clip(raised(values, jax.random.fold_in(stream_key, 3), *heavy), -bound, bound).astype(kind)


def setup_inputs(seed: int = 0) -> dict:
    key_of = jax.random.split(jax.random.key(seed), 8)
    return {
        "picture_tower_summary": heavy_noise(key_of[0], (TOKENS, WIDTH), 1.0, 24.0, ((0, 128),), (0, 1, 128, 5.5)),
        "caption_tower_summary": heavy_noise(key_of[1], (TOKENS, WIDTH), 1.0, 24.0, ((0, 128),), (0, 1, 128, 5.5)),
        "picture_head_matrix": scatter_about(key_of[2], (WIDTH, EMBED), (WIDTH * EMBED) ** -0.5, 0.00390625, ((1, 2),)),
        "caption_head_matrix": scatter_about(key_of[3], (WIDTH, EMBED), (WIDTH * EMBED) ** -0.5, 0.00390625, ((1, 2),)),
        "matching_caption_row": jax.vmap(lambda own: jax.random.permutation(own, ROWS))(jax.random.split(key_of[4], BLOCKS)).reshape((BLOCKS, ROWS)).astype(jnp.int32),
        "affinity_scale": jnp.clip(jnp.exp(jax.random.uniform(key_of[5], (1,), jnp.float32, math.log(4.0), math.log(16.0))), 4.0, 16.0),
        "affinity_offset": jnp.clip(jax.random.uniform(key_of[6], (1,), jnp.float32, -4.0, -2.0), -4.0, -2.0),
    }


def embed(features, projection):
    raw = jnp.dot(features, projection, preferred_element_type=jnp.float32)
    inverse = lax.rsqrt(lax.optimization_barrier(jnp.sum(raw * raw, axis=1, keepdims=True)) + 1e-06)
    return ((raw * inverse).astype(jnp.bfloat16), inverse)

def backward(emb, grad, inverse, features):
    emb_wide = emb.astype(jnp.float32)
    back = ((grad - emb_wide * lax.optimization_barrier(jnp.sum(emb_wide * grad, axis=1, keepdims=True))) * inverse).astype(jnp.bfloat16)
    return jnp.dot(features.T, back, preferred_element_type=jnp.float32)

def reference(picture_tower_summary, caption_tower_summary, picture_head_matrix, caption_head_matrix, matching_caption_row, affinity_scale, affinity_offset):
    image_emb, image_inv = embed(picture_tower_summary, picture_head_matrix)
    text_emb, text_inv = embed(caption_tower_summary, caption_head_matrix)
    image_block_list = image_emb.astype(jnp.float32).reshape(BLOCKS, ROWS, EMBED)
    text_blocks = text_emb.astype(jnp.float32).reshape(BLOCKS, ROWS, EMBED)
    steepness_multiplier = affinity_scale[0]
    shifted_bias = affinity_offset[0]
    positive = (jnp.arange(ROWS, dtype=jnp.int32)[None, None, :] == matching_caption_row[:, :, None]).astype(jnp.float32)
    losses = jnp.zeros((BLOCKS, ROWS), jnp.float32)
    image_gradient_sum = jnp.zeros((BLOCKS, ROWS, EMBED), jnp.float32)
    text_gradient_sum = jnp.zeros((BLOCKS, ROWS, EMBED), jnp.float32)
    for block_shift in range(-REACH, REACH + 1):
        neighbour_blocks = jnp.roll(text_blocks, -block_shift, axis=0)
        pair_logits = steepness_multiplier * jnp.einsum('dcm,dlm->dcl', image_block_list, neighbour_blocks) + shifted_bias
        labels = positive if block_shift == 0 else jnp.zeros_like(positive)
        losses = losses + lax.optimization_barrier(jnp.sum(jax.nn.softplus(pair_logits) - labels * pair_logits, axis=2))
        logit_slopes = lax.optimization_barrier(((jax.nn.sigmoid(pair_logits) - labels) / ROWS).astype(jnp.bfloat16)).astype(jnp.float32)
        image_gradient_sum = image_gradient_sum + steepness_multiplier * jnp.einsum('bqo,bof->bqf', logit_slopes, neighbour_blocks)
        text_gradient_sum = text_gradient_sum + jnp.roll(steepness_multiplier * jnp.einsum('bog,boq->bgq', logit_slopes, image_block_list), block_shift, axis=0)
    image_loss = (losses / ROWS).reshape(TOKENS)
    image_grad_w = backward(image_emb, image_gradient_sum.reshape(TOKENS, EMBED), image_inv, picture_tower_summary)
    text_grad_w = backward(text_emb, text_gradient_sum.reshape(TOKENS, EMBED), text_inv, caption_tower_summary)
    return (image_loss, image_grad_w, text_grad_w)
```

```python
import functools

import jax
import jax.numpy as jnp
import numpy as np
from jax import lax
from jax.experimental import pallas as pl
from jax.experimental.pallas import tpu as pltpu
from jax.sharding import PartitionSpec as P

MESH = pl.DeviceIdType.MESH
REACH = 4
XS, YS, ZS = 4, 2, 8
GROUP = 2 * YS


def column_order():
    order = np.arange(XS * YS * ZS * 2 * 12).reshape(XS, YS, ZS, 2, 12)
    return order.transpose(1, 3, 0, 2, 4).reshape(1, -1).astype(np.int32)


def weight_kernel(
    picture_ref, caption_ref, image_ref, text_ref, order_ref, image_out, text_out,
    towers_out, towers, backs, total, x_out, x_in, z_own, z_out, z_in, send, recv,
):
    dp, side = lax.axis_index("dp"), lax.axis_index("head")
    core = lax.rem(dp, 2)
    z = lax.rem(lax.div(dp, 2), ZS)
    y = lax.rem(lax.div(dp, 2 * ZS), YS)
    x = lax.div(dp, 2 * ZS * YS)

    def place(x, y, z, core):
        return ((x * YS + y) * ZS + z) * 2 + core

    sibling = (place(x, y, z, 1 - core), side)
    over = (place(x, 1 - y, z, core), side)
    crossed = [(place(x, 1 - y, z, c), 1 - side) for c in range(2)]
    x_peers = [(place(lax.rem(x + d, XS), y, z, core), side) for d in range(1, XS)]
    z_peers = [(place(x, y, lax.rem(z + d, ZS), core), side) for d in range(1, ZS)]
    greeted = [sibling, over, *crossed, *x_peers, *z_peers]
    barrier = pltpu.get_barrier_semaphore()
    for peer in greeted:
        pl.semaphore_signal(barrier, inc=1, device_id=peer, device_id_type=MESH)

    mine = y * 2 + core
    columns = order_ref.shape[1]
    part = columns // GROUP
    rows = picture_ref.shape[0]
    pair = jnp.concatenate([picture_ref[...], caption_ref[...]], axis=0)
    wide = columns // XS
    for g in range(GROUP):
        pick = order_ref[:, g * part : (g + 1) * part]
        acc = None
        for b in range(XS):
            chosen = (lax.broadcasted_iota(jnp.int32, (wide, part), 0) + b * wide == pick)
            one = jnp.where(chosen, 1.0, 0.0).astype(jnp.bfloat16)
            term = jnp.dot(pair[:, b * wide : (b + 1) * wide], one, preferred_element_type=jnp.float32)
            acc = term if acc is None else acc + term
        towers_out[g, 0] = acc[:rows].astype(jnp.bfloat16)
        towers_out[g, 1] = acc[rows:].astype(jnp.bfloat16)
    towers[mine] = towers_out[mine]
    backs[0, mine] = image_ref[...]
    backs[1, mine] = text_ref[...]

    pl.semaphore_wait(barrier, len(greeted))

    used = [0]

    def copy(src, dst, peer, arrival=None):
        at = used[0]
        used[0] += 1
        made = pltpu.make_async_remote_copy(
            src_ref=src, dst_ref=dst, send_sem=send.at[at],
            recv_sem=recv.at[at if arrival is None else arrival],
            device_id=peer, device_id_type=MESH,
        )
        made.start()
        return made

    def landed(dst, arrival):
        pltpu.make_async_copy(dst, dst, recv.at[arrival]).wait()

    cross_slot = (1 - y) * 2
    first = []
    for t in range(2):
        first.append((
            copy(backs.at[t, mine], backs.at[t, mine], over),
            copy(backs.at[t, mine], backs.at[t, mine], sibling),
        ))
    moved = [copy(towers_out.at[y * 2 + 1 - core], towers.at[mine], sibling)]
    base = used[0]
    for c in range(2):
        moved.append(copy(towers_out.at[cross_slot + c], towers.at[mine], crossed[c], base + core))
    passed = []
    for t in range(2):
        first[t][0].wait_recv()
        far = cross_slot + core
        passed.append(copy(backs.at[t, far], backs.at[t, far], sibling))
    moved[0].wait_recv()
    for c in range(2):
        landed(towers.at[cross_slot + c], base + c)
    spread = []
    for t in range(2):
        first[t][1].wait_recv()
        passed[t].wait_recv()
        left = towers[:, t].reshape(GROUP * rows, part)
        right = backs[t].reshape(GROUP * rows, backs.shape[3])
        product = lax.dot_general(left, right, (((0,), (0,)), ((), ())), preferred_element_type=jnp.float32)
        product = product.reshape(XS, part // XS, backs.shape[3])
        total[t] = product
        x_out[t] = product.astype(jnp.bfloat16)
        row = []
        for d in range(1, XS):
            row.append(copy(x_out.at[t, lax.rem(x + d, XS)], x_in.at[t, d - 1], x_peers[d - 1]))
        spread.append(row)
    last = []
    for t in range(2):
        value = total[t, x]
        for d in range(XS - 1):
            spread[t][d].wait_recv()
            value = value + x_in[t, d].astype(jnp.float32)
        for c in range(ZS):
            chunk = value[c * 12 : (c + 1) * 12]
            chunk = jnp.concatenate([chunk, jnp.zeros((4, chunk.shape[1]), jnp.float32)], axis=0)
            z_own[t, c] = chunk
            z_out[t, c] = chunk.astype(jnp.bfloat16)
        row = []
        for d in range(1, ZS):
            row.append(copy(z_out.at[t, lax.rem(z + d, ZS)], z_in.at[t, d - 1], z_peers[d - 1]))
        last.append(row)
    for t, out in ((0, image_out), (1, text_out)):
        value = z_own[t, z]
        for d in range(ZS - 1):
            last[t][d].wait_recv()
            value = value + z_in[t, d].astype(jnp.float32)
        out[...] = value[:12]
    for group in (*first, moved, passed, *spread, *last):
        for m in group:
            m.wait_send()


def weight_grads(picture, caption, back_image, back_text):
    rows, columns = picture.shape
    half = back_image.shape[1]
    part = columns // GROUP
    bf, f32 = jnp.bfloat16, jnp.float32
    copies = 4 + 3 + 2 + 2 * (XS - 1) + 2 * (ZS - 1)
    vmem = pl.BlockSpec(memory_space=pltpu.VMEM)
    return pl.pallas_call(
        weight_kernel,
        out_shape=[jax.ShapeDtypeStruct((12, half), f32)] * 2,
        in_specs=[vmem] * 5,
        out_specs=[vmem] * 2,
        scratch_shapes=[
            pltpu.VMEM((GROUP, 2, rows, part), bf),
            pltpu.VMEM((GROUP, 2, rows, part), bf),
            pltpu.VMEM((2, GROUP, rows, half), bf),
            pltpu.VMEM((2, XS, part // XS, half), f32),
            pltpu.VMEM((2, XS, part // XS, half), bf),
            pltpu.VMEM((2, XS - 1, part // XS, half), bf),
            pltpu.VMEM((2, ZS, 16, half), f32),
            pltpu.VMEM((2, ZS, 16, half), bf),
            pltpu.VMEM((2, ZS - 1, 16, half), bf),
            pltpu.SemaphoreType.DMA((copies,)),
            pltpu.SemaphoreType.DMA((copies,)),
        ],
        compiler_params=pltpu.CompilerParams(
            collective_id=0, has_side_effects=True, vmem_limit_bytes=48 * 1024 * 1024
        ),
    )(picture, caption, back_image, back_text, jnp.asarray(column_order()))


def shifted(value, axis, by):
    peers = lax.axis_size(axis)
    return lax.ppermute(value, axis, [(i, (i + by) % peers) for i in range(peers)])


def embed(features, projection):
    return jnp.dot(features, projection, preferred_element_type=jnp.float32)


def send_home(terms, distance):
    return shifted(terms, "dp", distance)


def shards(
    picture_tower_summary,
    caption_tower_summary,
    picture_head_matrix,
    caption_head_matrix,
    matching_caption_row,
    affinity_scale,
    affinity_offset,
):
    batch_rows = picture_tower_summary.shape[0]
    raw_image = embed(picture_tower_summary, picture_head_matrix)
    raw_text = embed(caption_tower_summary, caption_head_matrix)
    image_sq, text_sq = lax.psum(
        (jnp.sum(raw_image * raw_image, axis=1), jnp.sum(raw_text * raw_text, axis=1)), "head"
    )
    image_inv = lax.rsqrt(image_sq + 1e-06)[:, None]
    text_inv = lax.rsqrt(text_sq + 1e-06)[:, None]
    image_emb = (raw_image * image_inv).astype(jnp.bfloat16)
    text_emb = (raw_text * text_inv).astype(jnp.bfloat16)
    steepness_multiplier = affinity_scale[0]
    shifted_bias = affinity_offset[0]
    positive = (
        lax.broadcasted_iota(jnp.int32, (batch_rows, batch_rows), 1)
        == matching_caption_row[0][:, None]
    ).astype(jnp.float32)
    contract_last = (((1,), (1,)), ((), ()))
    contract_first = (((0,), (0,)), ((), ()))

    def visit(block, labels):
        partial_value = lax.dot_general(
            image_emb, block, contract_last, preferred_element_type=jnp.float32
        )
        pair_logits = steepness_multiplier * lax.psum(partial_value, "head") + shifted_bias
        loss_rows = jnp.sum(jax.nn.softplus(pair_logits) - labels * pair_logits, axis=1)
        logit_slopes = ((jax.nn.sigmoid(pair_logits) - labels) / batch_rows).astype(jnp.bfloat16)
        image_term = steepness_multiplier * jnp.dot(
            logit_slopes, block, preferred_element_type=jnp.float32
        )
        text_term = steepness_multiplier * lax.dot_general(
            logit_slopes, image_emb, contract_first, preferred_element_type=jnp.float32
        )
        return (loss_rows, image_term, text_term)

    loss_sum, image_gradient_sum, text_gradient_sum = visit(text_emb, positive)
    rising = text_emb
    falling = text_emb
    for hop_index in range(1, REACH + 1):
        rising = shifted(rising, "dp", -1)
        falling = shifted(falling, "dp", 1)
        loss_upper, image_upper, text_upper = visit(rising, 0.0)
        loss_lower, image_lower, text_lower = visit(falling, 0.0)
        loss_sum = loss_sum + loss_upper + loss_lower
        image_gradient_sum = image_gradient_sum + image_upper + image_lower
        text_gradient_sum = (
            text_gradient_sum + send_home(text_upper, hop_index) + send_home(text_lower, -hop_index)
        )
    image_wide = image_emb.astype(jnp.float32)
    text_wide = text_emb.astype(jnp.float32)
    image_dot, text_dot = lax.psum(
        (
            jnp.sum(image_wide * image_gradient_sum, axis=1),
            jnp.sum(text_wide * text_gradient_sum, axis=1),
        ),
        "head",
    )
    back_image = ((image_gradient_sum - image_wide * image_dot[:, None]) * image_inv).astype(
        jnp.bfloat16
    )
    back_text = ((text_gradient_sum - text_wide * text_dot[:, None]) * text_inv).astype(
        jnp.bfloat16
    )
    image_grad_w, text_grad_w = weight_grads(
        picture_tower_summary, caption_tower_summary, back_image, back_text
    )
    image_loss = loss_sum / batch_rows
    return (image_loss, image_grad_w, text_grad_w)


def solution(mesh):
    return jax.shard_map(
        shards,
        mesh=mesh,
        in_specs=(
            P("dp", None),
            P("dp", None),
            P(None, "head"),
            P(None, "head"),
            P("dp", None),
            P(),
            P(),
        ),
        out_specs=(P("dp"), P("dp", "head"), P("dp", "head")),
        check_vma=False,
    )
```

```python
import jax
import jax.numpy as jnp
import numpy as np
from jax import lax
from jax.experimental import pallas as pl
from jax.experimental.pallas import tpu as pltpu
from jax.sharding import PartitionSpec as P

MESH = pl.DeviceIdType.MESH
REACH = 4
XS, YS, ZS = 4, 2, 8
GROUP = 2 * YS
MET = 2 * REACH + 1
EXTRA = 16
COPIES = 2 + 8 + 8 + MET + 2 * REACH + 3 + 6 + 2 * (XS - 1) + 2 * (ZS - 1)
LAST = (((1,), (1,)), ((), ()))
FIRST = (((0,), (0,)), ((), ()))
F32, BF16 = jnp.float32, jnp.bfloat16


def column_order():
    order = np.arange(XS * YS * ZS * 2 * 12).reshape(XS, YS, ZS, 2, 12)
    return order.transpose(1, 3, 0, 2, 4).reshape(1, -1).astype(np.int32)


def as_row(column):
    n = column.shape[0]
    return jnp.transpose(jnp.broadcast_to(column, (n, n)))[:8]


def as_column(row):
    n = row.shape[1]
    return jnp.transpose(jnp.broadcast_to(row, (n, n)))[:, :1]


def kernel(
    picture_ref, caption_ref, picture_head_hbm, caption_head_hbm, match_ref, scale_ref, offset_ref, order_ref,
    loss_out, image_out, text_out,
    picture_head, caption_head, raws, norm_out, norm_in, texts, images, part_out, part_in, slope_out, slope_in,
    loss_sum, dot_sum, towers_out, towers, backs, total, x_out, x_in, z_own, z_out, z_in, load, send, recv,
):
    dp, side = lax.axis_index("dp"), lax.axis_index("head")
    core = lax.rem(dp, 2)
    z = lax.rem(lax.div(dp, 2), ZS)
    y = lax.rem(lax.div(dp, 2 * ZS), YS)
    x = lax.div(dp, 2 * ZS * YS)
    blocks = XS * YS * ZS * 2
    rows, columns = picture_ref.shape
    half = picture_head.shape[1]

    head_loads = [
        pltpu.make_async_copy(caption_head_hbm, caption_head, load.at[0]),
        pltpu.make_async_copy(picture_head_hbm, picture_head, load.at[1]),
    ]
    for copy_in in head_loads:
        copy_in.start()

    def place(x, y, z, core):
        return ((x * YS + y) * ZS + z) * 2 + core

    def block(by):
        return (lax.rem(dp + by + blocks, blocks), side)

    peer = (dp, 1 - side)
    sibling = (dp + 1 - 2 * core, side)
    over = (place(x, 1 - y, z, core), side)
    crossed = [(place(x, 1 - y, z, c), 1 - side) for c in range(2)]
    x_peers = [(place(lax.rem(x + d, XS), y, z, core), side) for d in range(1, XS)]
    z_peers = [(place(x, y, lax.rem(z + d, ZS), core), side) for d in range(1, ZS)]
    near = [block(by) for by in range(-REACH, REACH + 1) if by]
    greeted = [peer, over, *crossed, *near, *x_peers, *z_peers]
    barrier = pltpu.get_barrier_semaphore()
    for other in greeted:
        pl.semaphore_signal(barrier, inc=1, device_id=other, device_id_type=MESH)

    used = [0]
    sent = []

    def copy(src, dst, target, arrival=None):
        at = used[0]
        used[0] += 1
        at_arrival = at if arrival is None else arrival
        made = pltpu.make_async_remote_copy(
            src_ref=src, dst_ref=dst, send_sem=send.at[at], recv_sem=recv.at[at_arrival],
            device_id=target, device_id_type=MESH,
        )
        made.start()
        sent.append(made)
        return at

    def landed(dst, at):
        pltpu.make_async_copy(dst, dst, recv.at[at]).wait()

    norm_at = []
    for t, tower_ref, head in ((0, caption_ref, caption_head), (1, picture_ref, picture_head)):
        head_loads[t].wait()
        raw = jnp.dot(tower_ref[...], head[...], preferred_element_type=F32)
        raws[t] = raw
        norm_out[t] = as_row(jnp.sum(raw * raw, axis=1, keepdims=True))
        if t == 0:
            pl.semaphore_wait(barrier, len(greeted))
        norm_at.append(copy(norm_out.at[t], norm_in.at[t], peer))

    def embedding(t):
        landed(norm_in.at[t], norm_at[t])
        inverse = lax.rsqrt(as_column((norm_out[t] + norm_in[t])[:1]) + 1e-06)
        return (raws[t] * inverse).astype(BF16), inverse

    def spread_own(held):
        at = {by: copy(held.at[REACH], held.at[REACH - by], block(by)) for by in (2, -2, 4, -4)}
        at["own"] = copy(held.at[REACH], held.at[REACH + 2 * core - 1], sibling)
        return at

    def arrived(held, at, by):
        landed(held.at[REACH + by], at[-by])

    def hand_over(held, at, name, by):
        at[name] = copy(held.at[REACH + by], held.at[REACH + by - 1 + 2 * core], sibling)

    outer = 4 - 8 * core
    slot_of = {
        "own": REACH + 1 - 2 * core,
        "up": REACH + 3 - 2 * core,
        "down": REACH - 1 - 2 * core,
        "outer": REACH - 3 + 6 * core,
    }

    text_emb, text_inv = embedding(0)
    texts[REACH] = text_emb
    text_at = spread_own(texts)
    image_emb, image_inv = embedding(1)
    images[REACH] = image_emb

    part_at = {}

    def logits(key, slot):
        part_out[slot] = lax.dot_general(images[REACH], texts[slot], LAST, preferred_element_type=F32)
        part_at[key] = copy(part_out.at[slot], part_in.at[slot], peer)

    logits(0, REACH)

    mine = y * 2 + core
    part = columns // GROUP
    wide = columns // XS
    pair = jnp.concatenate([picture_ref[...], caption_ref[...]], axis=0)
    for g in range(GROUP):
        pick = order_ref[:, g * part : (g + 1) * part]
        acc = None
        for b in range(XS):
            chosen = lax.broadcasted_iota(jnp.int32, (wide, part), 0) + b * wide == pick
            one = jnp.where(chosen, 1.0, 0.0).astype(BF16)
            term = jnp.dot(pair[:, b * wide : (b + 1) * wide], one, preferred_element_type=F32)
            acc = term if acc is None else acc + term
        towers_out[g, 0] = acc[:rows].astype(BF16)
        towers_out[g, 1] = acc[rows:].astype(BF16)
    towers[mine] = towers_out[mine]
    cross_slot = (1 - y) * 2
    tower_at = copy(towers_out.at[y * 2 + 1 - core], towers.at[mine], sibling)
    cross_at = used[0]
    for c in range(2):
        copy(towers_out.at[cross_slot + c], towers.at[mine], crossed[c], cross_at + core)

    landed(texts.at[slot_of["own"]], text_at["own"])
    logits("own", slot_of["own"])
    image_at = spread_own(images)

    scale, offset = scale_ref[0], offset_ref[0]
    match = as_column(match_ref[...].astype(F32))
    positive = jnp.where(
        lax.broadcasted_iota(jnp.int32, (rows, rows), 1).astype(F32) == match, 1.0, 0.0
    )
    slope_at = {}

    def slopes(key, slot, by):
        landed(part_in.at[slot], part_at[key])
        product = scale * (part_out[slot] + part_in[slot])
        logit = product + offset
        small = jnp.exp(-jnp.abs(logit))
        inverse = 1.0 / (1.0 + small)
        sigmoid = jnp.where(logit >= 0.0, inverse, small * inverse)
        loss = jnp.maximum(logit, 0.0) + jnp.log1p(small)
        if key == 0:
            sigmoid = sigmoid - positive
            loss = loss - positive * logit
        slope = (sigmoid * (1.0 / rows)).astype(BF16)
        weighted = slope.astype(F32) * product
        if key == 0:
            loss_sum[...] = loss
            dot_sum[...] = weighted
        else:
            loss_sum[...] += loss
            dot_sum[...] += weighted
        over_images = jnp.sum(weighted, axis=0, keepdims=True)
        high = over_images.astype(BF16).astype(F32)
        middle = (over_images - high).astype(BF16).astype(F32)
        low = over_images - high - middle
        extra = jnp.concatenate([high, middle, low, jnp.zeros((EXTRA - 3, rows), F32)], axis=0)
        slope_out[slot, :rows] = slope
        slope_out[slot, rows:] = extra.astype(BF16)
        if key == 0:
            slope_in[REACH] = slope_out[REACH]
        else:
            slope_at[key] = copy(slope_out.at[slot], slope_in.at[2 * REACH - slot], block(by))

    slopes(0, REACH, 0)
    for name, by in (("up", 2), ("down", -2)):
        arrived(texts, text_at, by)
        hand_over(texts, text_at, name, by)
        logits(by, REACH + by)
    slopes("own", slot_of["own"], 1 - 2 * core)
    for by in (4, -4):
        arrived(texts, text_at, by)
        logits(by, REACH + by)
    hand_over(texts, text_at, "outer", outer)
    for name in ("up", "down"):
        landed(texts.at[slot_of[name]], text_at[name])
        logits(name, slot_of[name])
    for by in (2, -2):
        slopes(by, REACH + by, by)
    for name, by in (("up", 2), ("down", -2)):
        arrived(images, image_at, by)
        hand_over(images, image_at, name, by)
    for by in (4, -4):
        slopes(by, REACH + by, by)
    landed(texts.at[slot_of["outer"]], text_at["outer"])
    logits("outer", slot_of["outer"])
    for name in ("up", "down"):
        slopes(name, slot_of[name], slot_of[name] - REACH)
    for by in (4, -4):
        arrived(images, image_at, by)
    hand_over(images, image_at, "outer", outer)
    slopes("outer", slot_of["outer"], slot_of["outer"] - REACH)

    def back_through(gradient, emb, dot, inverse):
        return ((scale * gradient - emb.astype(F32) * dot) * inverse).astype(BF16)

    across = jnp.concatenate([slope_out[k, :rows] for k in range(MET)], axis=1)
    gradient = jnp.dot(across, texts[...].reshape(MET * rows, half), preferred_element_type=F32)
    image_dot = jnp.sum(dot_sum[...], axis=1, keepdims=True)
    backs[0, mine] = back_through(gradient, images[REACH], image_dot, image_inv)
    back_at = {}

    def spread_back(t):
        back_at[t, "over"] = copy(backs.at[t, mine], backs.at[t, mine], over)
        back_at[t, "sibling"] = copy(backs.at[t, mine], backs.at[t, mine], sibling)

    spread_back(0)
    loss_out[...] = as_row(jnp.sum(loss_sum[...], axis=1, keepdims=True))[:1] * (1.0 / rows)

    came = {-2: -2, 2: 2, -4: -4, 4: 4, "own": None, "up": None, "down": None, "outer": None}
    slope_slot = {
        "own": REACH + 1 - 2 * core,
        "up": REACH - 1 - 2 * core,
        "down": REACH + 3 - 2 * core,
        "outer": REACH - 3 + 6 * core,
    }
    for name in came:
        slot = REACH - name if came[name] else slope_slot[name]
        landed(slope_in.at[slot], slope_at[name])
    for name in slot_of:
        landed(images.at[slot_of[name]], image_at[name])
    text_dot = None
    for k in range(MET):
        rows3 = jnp.sum(slope_in[k, rows:].astype(F32), axis=0, keepdims=True)
        text_dot = rows3 if text_dot is None else text_dot + rows3
    down = jnp.concatenate([slope_in[k, :rows] for k in range(MET)], axis=0)
    gradient = lax.dot_general(
        down, images[...].reshape(MET * rows, half), FIRST, preferred_element_type=F32
    )
    backs[1, mine] = back_through(gradient, texts[REACH], as_column(text_dot), text_inv)
    spread_back(1)

    far = cross_slot + core
    for t in range(2):
        landed(backs.at[t, far], back_at[t, "over"])
        back_at[t, "passed"] = copy(backs.at[t, far], backs.at[t, far], sibling)
    landed(towers.at[y * 2 + 1 - core], tower_at)
    for c in range(2):
        landed(towers.at[cross_slot + c], cross_at + c)
    x_at = {}
    for t in range(2):
        landed(backs.at[t, y * 2 + 1 - core], back_at[t, "sibling"])
        landed(backs.at[t, cross_slot + 1 - core], back_at[t, "passed"])
        product = lax.dot_general(
            towers[:, t].reshape(GROUP * rows, part), backs[t].reshape(GROUP * rows, half),
            FIRST, preferred_element_type=F32,
        ).reshape(XS, part // XS, half)
        total[t] = product
        x_out[t] = product.astype(BF16)
        for d in range(1, XS):
            x_at[t, d] = copy(x_out.at[t, lax.rem(x + d, XS)], x_in.at[t, d - 1], x_peers[d - 1])
    z_at = {}
    for t in range(2):
        value = total[t, x]
        for d in range(1, XS):
            landed(x_in.at[t, d - 1], x_at[t, d])
            value = value + x_in[t, d - 1].astype(F32)
        for c in range(ZS):
            chunk = value[c * 12 : (c + 1) * 12]
            chunk = jnp.concatenate([chunk, jnp.zeros((4, half), F32)], axis=0)
            z_own[t, c] = chunk
            z_out[t, c] = chunk.astype(BF16)
        for d in range(1, ZS):
            z_at[t, d] = copy(z_out.at[t, lax.rem(z + d, ZS)], z_in.at[t, d - 1], z_peers[d - 1])
    for t, out in ((0, image_out), (1, text_out)):
        value = z_own[t, z]
        for d in range(1, ZS):
            landed(z_in.at[t, d - 1], z_at[t, d])
            value = value + z_in[t, d - 1].astype(F32)
        out[...] = value[:12]
    for made in sent:
        made.wait_send()


def shards(
    picture_tower_summary,
    caption_tower_summary,
    picture_head_matrix,
    caption_head_matrix,
    matching_caption_row,
    affinity_scale,
    affinity_offset,
):
    rows, columns = picture_tower_summary.shape
    half = picture_head_matrix.shape[1]
    part = columns // GROUP
    vmem = pl.BlockSpec(memory_space=pltpu.VMEM)
    smem = pl.BlockSpec(memory_space=pltpu.SMEM)
    hbm = pl.BlockSpec(memory_space=pl.ANY)
    loss, image_grad_w, text_grad_w = pl.pallas_call(
        kernel,
        out_shape=[
            jax.ShapeDtypeStruct((1, rows), F32),
            jax.ShapeDtypeStruct((12, half), F32),
            jax.ShapeDtypeStruct((12, half), F32),
        ],
        in_specs=[vmem, vmem, hbm, hbm, vmem, smem, smem, vmem],
        out_specs=[vmem] * 3,
        scratch_shapes=[
            pltpu.VMEM((columns, half), BF16),
            pltpu.VMEM((columns, half), BF16),
            pltpu.VMEM((2, rows, half), F32),
            pltpu.VMEM((2, 8, rows), F32),
            pltpu.VMEM((2, 8, rows), F32),
            pltpu.VMEM((MET, rows, half), BF16),
            pltpu.VMEM((MET, rows, half), BF16),
            pltpu.VMEM((MET, rows, rows), F32),
            pltpu.VMEM((MET, rows, rows), F32),
            pltpu.VMEM((MET, rows + EXTRA, rows), BF16),
            pltpu.VMEM((MET, rows + EXTRA, rows), BF16),
            pltpu.VMEM((rows, rows), F32),
            pltpu.VMEM((rows, rows), F32),
            pltpu.VMEM((GROUP, 2, rows, part), BF16),
            pltpu.VMEM((GROUP, 2, rows, part), BF16),
            pltpu.VMEM((2, GROUP, rows, half), BF16),
            pltpu.VMEM((2, XS, part // XS, half), F32),
            pltpu.VMEM((2, XS, part // XS, half), BF16),
            pltpu.VMEM((2, XS - 1, part // XS, half), BF16),
            pltpu.VMEM((2, ZS, 16, half), F32),
            pltpu.VMEM((2, ZS, 16, half), BF16),
            pltpu.VMEM((2, ZS - 1, 16, half), BF16),
            pltpu.SemaphoreType.DMA((2,)),
            pltpu.SemaphoreType.DMA((COPIES,)),
            pltpu.SemaphoreType.DMA((COPIES,)),
        ],
        compiler_params=pltpu.CompilerParams(
            collective_id=0, has_side_effects=True, vmem_limit_bytes=56 * 1024 * 1024
        ),
    )(
        picture_tower_summary, caption_tower_summary, picture_head_matrix, caption_head_matrix,
        matching_caption_row, affinity_scale, affinity_offset, jnp.asarray(column_order()),
    )
    return loss[0], image_grad_w, text_grad_w


def solution(mesh):
    return jax.shard_map(
        shards,
        mesh=mesh,
        in_specs=(
            P("dp", None),
            P("dp", None),
            P(None, "head"),
            P(None, "head"),
            P("dp", None),
            P(),
            P(),
        ),
        out_specs=(P("dp"), P("dp", "head"), P("dp", "head")),
        check_vma=False,
    )
```

```python
import jax
import jax.numpy as jnp
import numpy as np
from jax import lax
from jax.experimental import pallas as pl
from jax.experimental.pallas import tpu as pltpu
from jax.sharding import PartitionSpec as P

MESH = pl.DeviceIdType.MESH
REACH = 4
XS, YS, ZS = 4, 2, 8
GROUP = 2 * YS
MET = 2 * REACH + 1
EXTRA = 16
CHUNKS = 2
COPIES = 2 + 2 * (7 * CHUNKS + 1) + MET + 2 * REACH + 3 + 12 + 4 * (XS - 1) + 4 * (ZS - 1)
PARTS = 32000.0
LAST = (((1,), (1,)), ((), ()))
FIRST = (((0,), (0,)), ((), ()))
F32, BF16 = jnp.float32, jnp.bfloat16


def column_order():
    order = np.arange(XS * YS * ZS * 2 * 12).reshape(XS, YS, ZS, 2, 12)
    return order.transpose(1, 3, 0, 2, 4).reshape(1, -1).astype(np.int32)


def as_row(column):
    n = column.shape[0]
    return jnp.transpose(jnp.broadcast_to(column, (n, n)))[:8]


def as_column(row):
    n = row.shape[1]
    return jnp.transpose(jnp.broadcast_to(row, (n, n)))[:, :1]


def kernel(
    picture_hbm, caption_hbm, picture_head_hbm, caption_head_hbm, match_ref, scale_ref, offset_ref, order_ref,
    loss_out, image_out, text_out,
    picture_ref, caption_ref, picture_head, caption_head, raws, norm_out, norm_in, texts, images, part_own, part_out, part_in, slope_out, slope_in,
    loss_sum, dot_sum, towers_out, towers, backs, total, x_out, x_in, z_own, z_out, z_in, load, send, recv,
):
    dp, side = lax.axis_index("dp"), lax.axis_index("head")
    core = lax.rem(dp, 2)
    z = lax.rem(lax.div(dp, 2), ZS)
    y = lax.rem(lax.div(dp, 2 * ZS), YS)
    x = lax.div(dp, 2 * ZS * YS)
    blocks = XS * YS * ZS * 2
    rows, columns = picture_ref.shape
    half = picture_head.shape[1]

    loads = [
        pltpu.make_async_copy(caption_hbm, caption_ref, load.at[0]),
        pltpu.make_async_copy(caption_head_hbm, caption_head, load.at[1]),
        pltpu.make_async_copy(picture_hbm, picture_ref, load.at[2]),
        pltpu.make_async_copy(picture_head_hbm, picture_head, load.at[3]),
    ]
    for copy_in in loads:
        copy_in.start()

    def place(x, y, z, core):
        return ((x * YS + y) * ZS + z) * 2 + core

    def block(by):
        return (lax.rem(dp + by + blocks, blocks), side)

    peer = (dp, 1 - side)
    sibling = (dp + 1 - 2 * core, side)
    over = (place(x, 1 - y, z, core), side)
    crossed = [(place(x, 1 - y, z, c), 1 - side) for c in range(2)]
    x_peers = [(place(lax.rem(x + d, XS), y, z, core), side) for d in range(1, XS)]
    z_peers = [(place(x, y, lax.rem(z + d, ZS), core), side) for d in range(1, ZS)]
    near = [block(by) for by in range(-REACH, REACH + 1) if by]
    greeted = [peer, over, *crossed, *near, *x_peers, *z_peers]
    barrier = pltpu.get_barrier_semaphore()
    for other in greeted:
        pl.semaphore_signal(barrier, inc=1, device_id=other, device_id_type=MESH)

    mine = y * 2 + core
    cross_slot = (1 - y) * 2
    part = columns // GROUP
    wide = columns // XS
    cut = half // 2
    used = [0]
    sent = []

    def copy(src, dst, target, arrival=None):
        at = used[0]
        used[0] += 1
        at_arrival = at if arrival is None else arrival
        made = pltpu.make_async_remote_copy(
            src_ref=src, dst_ref=dst, send_sem=send.at[at], recv_sem=recv.at[at_arrival],
            device_id=target, device_id_type=MESH,
        )
        made.start()
        sent.append(made)
        return at

    def landed(dst, at):
        pltpu.make_async_copy(dst, dst, recv.at[at]).wait()

    norm_at = []
    for t, tower_ref, head in ((0, caption_ref, caption_head), (1, picture_ref, picture_head)):
        loads[2 * t].wait()
        loads[2 * t + 1].wait()
        raw = jnp.dot(tower_ref[...], head[...], preferred_element_type=F32)
        raws[t] = raw
        norm_out[t] = as_row(jnp.sum(raw * raw, axis=1, keepdims=True))
        if t == 0:
            pl.semaphore_wait(barrier, len(greeted))
        norm_at.append(copy(norm_out.at[t], norm_in.at[t], peer))

    def embedding(t):
        landed(norm_in.at[t], norm_at[t])
        inverse = lax.rsqrt(as_column((norm_out[t] + norm_in[t])[:1]) + 1e-06)
        return (raws[t] * inverse).astype(BF16), inverse

    size = rows // CHUNKS

    def piece(held, slot, c):
        return held.at[slot, pl.ds(c * size, size)]

    def spread_own(held):
        at = {}
        for c in range(CHUNKS):
            for by in (2, -2):
                at[by, c] = copy(piece(held, REACH, c), piece(held, REACH - by, c), block(by))
        at["own"] = copy(held.at[REACH], held.at[REACH + 2 * core - 1], sibling)
        return at

    def relay(held, at):
        for c in range(CHUNKS):
            for by in (2, -2):
                landed(piece(held, REACH - by, c), at[by, c])
                at["on", by, c] = copy(piece(held, REACH - by, c), piece(held, REACH - 2 * by, c), block(by))
            for name, by in (("up", 2), ("down", -2)):
                hand_over(held, at, name, by, c)

    def relayed(held, at):
        for c in range(CHUNKS):
            for by in (2, -2):
                landed(piece(held, REACH - 2 * by, c), at["on", by, c])
            hand_over(held, at, "outer", outer, c)

    def hand_over(held, at, name, by, c):
        at[name, c] = copy(piece(held, REACH + by, c), piece(held, REACH + by - 1 + 2 * core, c), sibling)

    def handed(held, at, name):
        for c in range(CHUNKS):
            landed(piece(held, slot_of[name], c), at[name, c])

    outer = 4 - 8 * core
    slot_of = {
        "own": REACH + 1 - 2 * core,
        "up": REACH + 3 - 2 * core,
        "down": REACH - 1 - 2 * core,
        "outer": REACH - 3 + 6 * core,
    }

    pair = jnp.concatenate([picture_ref[...], caption_ref[...]], axis=0)
    for g in range(GROUP):
        pick = order_ref[:, g * part : (g + 1) * part]
        acc = None
        for b in range(XS):
            chosen = lax.broadcasted_iota(jnp.int32, (wide, part), 0) + b * wide == pick
            one = jnp.where(chosen, 1.0, 0.0).astype(BF16)
            term = jnp.dot(pair[:, b * wide : (b + 1) * wide], one, preferred_element_type=F32)
            acc = term if acc is None else acc + term
        towers_out[g, 0] = acc[:rows].astype(BF16)
        towers_out[g, 1] = acc[rows:].astype(BF16)
    towers[mine] = towers_out[mine]
    tower_at = copy(towers_out.at[y * 2 + 1 - core], towers.at[mine], sibling)
    cross_at = used[0]
    for c in range(2):
        copy(towers_out.at[cross_slot + c], towers.at[mine], crossed[c], cross_at + core)


    text_emb, text_inv = embedding(0)
    texts[REACH] = text_emb
    text_at = spread_own(texts)
    image_emb, image_inv = embedding(1)
    images[REACH] = image_emb

    part_at = {}

    def logits(key, slot):
        value = lax.dot_general(images[REACH], texts[slot], LAST, preferred_element_type=F32)
        part_own[slot] = value
        part_out[slot] = jnp.round(value * PARTS).astype(jnp.int32).astype(jnp.int16)
        part_at[key] = copy(part_out.at[slot], part_in.at[slot], peer)

    scale, offset = scale_ref[0], offset_ref[0]
    match = as_column(match_ref[...].astype(F32))
    positive = jnp.where(
        lax.broadcasted_iota(jnp.int32, (rows, rows), 1).astype(F32) == match, 1.0, 0.0
    )
    slope_at = {}

    def slopes(key, slot, by):
        landed(part_in.at[slot], part_at[key])
        other = part_in[slot].astype(jnp.int32).astype(F32) * (1.0 / PARTS)
        product = scale * (part_own[slot] + other)
        logit = product + offset
        small = jnp.exp(-jnp.abs(logit))
        inverse = 1.0 / (1.0 + small)
        sigmoid = jnp.where(logit >= 0.0, inverse, small * inverse)
        loss = jnp.maximum(logit, 0.0) + jnp.log1p(small)
        if key == 0:
            sigmoid = sigmoid - positive
            loss = loss - positive * logit
        slope = (sigmoid * (1.0 / rows)).astype(BF16)
        weighted = slope.astype(F32) * product
        if key == 0:
            loss_sum[...] = loss
            dot_sum[...] = weighted
        else:
            loss_sum[...] += loss
            dot_sum[...] += weighted
        over_images = jnp.sum(weighted, axis=0, keepdims=True)
        high = over_images.astype(BF16).astype(F32)
        middle = (over_images - high).astype(BF16).astype(F32)
        low = over_images - high - middle
        extra = jnp.concatenate([high, middle, low, jnp.zeros((EXTRA - 3, rows), F32)], axis=0)
        slope_out[slot, :rows] = slope
        slope_out[slot, rows:] = extra.astype(BF16)
        if key == 0:
            slope_in[REACH] = slope_out[REACH]
        else:
            slope_at[key] = copy(slope_out.at[slot], slope_in.at[2 * REACH - slot], block(by))

    logits(0, REACH)
    landed(texts.at[slot_of["own"]], text_at["own"])
    logits("own", slot_of["own"])
    relay(texts, text_at)
    image_at = spread_own(images)
    for by in (2, -2):
        logits(by, REACH + by)
    slopes(0, REACH, 0)
    slopes("own", slot_of["own"], 1 - 2 * core)
    for name in ("up", "down"):
        handed(texts, text_at, name)
        logits(name, slot_of[name])
    relayed(texts, text_at)
    for by in (4, -4):
        logits(by, REACH + by)
    handed(texts, text_at, "outer")
    logits("outer", slot_of["outer"])
    relay(images, image_at)
    for by in (2, -2):
        slopes(by, REACH + by, by)
    for name in ("up", "down"):
        slopes(name, slot_of[name], slot_of[name] - REACH)
    for by in (4, -4):
        slopes(by, REACH + by, by)
    slopes("outer", slot_of["outer"], slot_of["outer"] - REACH)

    def back_through(gradient, emb, dot, inverse):
        return ((scale * gradient - emb.astype(F32) * dot) * inverse).astype(BF16)

    across = jnp.concatenate([slope_out[k, :rows] for k in range(MET)], axis=1)
    gradient = jnp.dot(across, texts[...].reshape(MET * rows, half), preferred_element_type=F32)
    image_dot = jnp.sum(dot_sum[...], axis=1, keepdims=True)
    back = back_through(gradient, images[REACH], image_dot, image_inv)
    back_at = {}

    def spread_back(t, back):
        for h in range(2):
            backs[t, h, mine] = back[:, h * cut : (h + 1) * cut]
            back_at[t, h, "over"] = copy(backs.at[t, h, mine], backs.at[t, h, mine], over)
        for h in range(2):
            back_at[t, h, "sibling"] = copy(backs.at[t, h, mine], backs.at[t, h, mine], sibling)

    spread_back(0, back)
    loss_out[...] = as_row(jnp.sum(loss_sum[...], axis=1, keepdims=True))[:1] * (1.0 / rows)

    relayed(images, image_at)

    came = {-2: -2, 2: 2, -4: -4, 4: 4, "own": None, "up": None, "down": None, "outer": None}
    slope_slot = {
        "own": REACH + 1 - 2 * core,
        "up": REACH - 1 - 2 * core,
        "down": REACH + 3 - 2 * core,
        "outer": REACH - 3 + 6 * core,
    }
    for name in came:
        slot = REACH - name if came[name] else slope_slot[name]
        landed(slope_in.at[slot], slope_at[name])
    landed(images.at[slot_of["own"]], image_at["own"])
    for name in ("up", "down", "outer"):
        handed(images, image_at, name)
    text_dot = None
    for k in range(MET):
        rows3 = jnp.sum(slope_in[k, rows:].astype(F32), axis=0, keepdims=True)
        text_dot = rows3 if text_dot is None else text_dot + rows3
    down = jnp.concatenate([slope_in[k, :rows] for k in range(MET)], axis=0)
    gradient = lax.dot_general(
        down, images[...].reshape(MET * rows, half), FIRST, preferred_element_type=F32
    )
    spread_back(1, back_through(gradient, texts[REACH], as_column(text_dot), text_inv))

    far = cross_slot + core
    landed(towers.at[y * 2 + 1 - core], tower_at)
    for c in range(2):
        landed(towers.at[cross_slot + c], cross_at + c)
    x_at = {}
    parts = [(t, h) for t in range(2) for h in range(2)]
    for t, h in parts:
        held = backs.at[t, h]
        landed(held.at[far], back_at[t, h, "over"])
        passed = copy(held.at[far], held.at[far], sibling)
        landed(held.at[y * 2 + 1 - core], back_at[t, h, "sibling"])
        landed(held.at[cross_slot + 1 - core], passed)
        product = lax.dot_general(
            towers[:, t].reshape(GROUP * rows, part), backs[t, h].reshape(GROUP * rows, cut),
            FIRST, preferred_element_type=F32,
        ).reshape(XS, part // XS, cut)
        total[t, h] = product
        x_out[t, h] = product.astype(BF16)
        for d in range(1, XS):
            x_at[t, h, d] = copy(x_out.at[t, h, lax.rem(x + d, XS)], x_in.at[t, h, d - 1], x_peers[d - 1])
    z_at = {}
    for t, h in parts:
        value = total[t, h, x]
        for d in range(1, XS):
            landed(x_in.at[t, h, d - 1], x_at[t, h, d])
            value = value + x_in[t, h, d - 1].astype(F32)
        for c in range(ZS):
            chunk = value[c * 12 : (c + 1) * 12]
            chunk = jnp.concatenate([chunk, jnp.zeros((4, cut), F32)], axis=0)
            z_own[t, h, c] = chunk
            z_out[t, h, c] = chunk.astype(BF16)
        for d in range(1, ZS):
            z_at[t, h, d] = copy(z_out.at[t, h, lax.rem(z + d, ZS)], z_in.at[t, h, d - 1], z_peers[d - 1])
    for t, h in parts:
        value = z_own[t, h, z]
        for d in range(1, ZS):
            landed(z_in.at[t, h, d - 1], z_at[t, h, d])
            value = value + z_in[t, h, d - 1].astype(F32)
        (image_out, text_out)[t][:, h * cut : (h + 1) * cut] = value[:12]
    for made in sent:
        made.wait_send()


def results(loss_ref, image_ref, text_ref, loss_out, image_out, text_out):
    loss_out[...] = loss_ref[...]
    image_out[...] = image_ref[...]
    text_out[...] = text_ref[...]


def shards(
    picture_tower_summary,
    caption_tower_summary,
    picture_head_matrix,
    caption_head_matrix,
    matching_caption_row,
    affinity_scale,
    affinity_offset,
):
    rows, columns = picture_tower_summary.shape
    half = picture_head_matrix.shape[1]
    part = columns // GROUP
    vmem = pl.BlockSpec(memory_space=pltpu.VMEM)
    smem = pl.BlockSpec(memory_space=pltpu.SMEM)
    hbm = pl.BlockSpec(memory_space=pl.ANY)
    loss, image_grad_w, text_grad_w = pl.pallas_call(
        kernel,
        out_shape=[
            jax.ShapeDtypeStruct((1, rows), F32),
            jax.ShapeDtypeStruct((12, half), F32),
            jax.ShapeDtypeStruct((12, half), F32),
        ],
        in_specs=[hbm, hbm, hbm, hbm, vmem, smem, smem, vmem],
        out_specs=[vmem] * 3,
        scratch_shapes=[
            pltpu.VMEM((rows, columns), BF16),
            pltpu.VMEM((rows, columns), BF16),
            pltpu.VMEM((columns, half), BF16),
            pltpu.VMEM((columns, half), BF16),
            pltpu.VMEM((2, rows, half), F32),
            pltpu.VMEM((2, 8, rows), F32),
            pltpu.VMEM((2, 8, rows), F32),
            pltpu.VMEM((MET, rows, half), BF16),
            pltpu.VMEM((MET, rows, half), BF16),
            pltpu.VMEM((MET, rows, rows), F32),
            pltpu.VMEM((MET, rows, rows), jnp.int16),
            pltpu.VMEM((MET, rows, rows), jnp.int16),
            pltpu.VMEM((MET, rows + EXTRA, rows), BF16),
            pltpu.VMEM((MET, rows + EXTRA, rows), BF16),
            pltpu.VMEM((rows, rows), F32),
            pltpu.VMEM((rows, rows), F32),
            pltpu.VMEM((GROUP, 2, rows, part), BF16),
            pltpu.VMEM((GROUP, 2, rows, part), BF16),
            pltpu.VMEM((2, 2, GROUP, rows, half // 2), BF16),
            pltpu.VMEM((2, 2, XS, part // XS, half // 2), F32),
            pltpu.VMEM((2, 2, XS, part // XS, half // 2), BF16),
            pltpu.VMEM((2, 2, XS - 1, part // XS, half // 2), BF16),
            pltpu.VMEM((2, 2, ZS, 16, half // 2), F32),
            pltpu.VMEM((2, 2, ZS, 16, half // 2), BF16),
            pltpu.VMEM((2, 2, ZS - 1, 16, half // 2), BF16),
            pltpu.SemaphoreType.DMA((4,)),
            pltpu.SemaphoreType.DMA((COPIES,)),
            pltpu.SemaphoreType.DMA((COPIES,)),
        ],
        compiler_params=pltpu.CompilerParams(
            collective_id=0, has_side_effects=True, vmem_limit_bytes=56 * 1024 * 1024
        ),
    )(
        picture_tower_summary, caption_tower_summary, picture_head_matrix, caption_head_matrix,
        matching_caption_row, affinity_scale, affinity_offset, jnp.asarray(column_order()),
    )
    loss, image_grad_w, text_grad_w = pl.pallas_call(
        results,
        out_shape=[
            jax.ShapeDtypeStruct((1, rows), F32),
            jax.ShapeDtypeStruct((12, half), F32),
            jax.ShapeDtypeStruct((12, half), F32),
        ],
        in_specs=[vmem] * 3,
        out_specs=[vmem] * 3,
    )(loss, image_grad_w, text_grad_w)
    return loss[0], image_grad_w, text_grad_w


def solution(mesh):
    return jax.shard_map(
        shards,
        mesh=mesh,
        in_specs=(
            P("dp", None),
            P("dp", None),
            P(None, "head"),
            P(None, "head"),
            P("dp", None),
            P(),
            P(),
        ),
        out_specs=(P("dp"), P("dp", "head"), P("dp", "head")),
        check_vma=False,
    )
```

```python
import jax
import jax.numpy as jnp
import numpy as np
from jax import lax
from jax.experimental import pallas as pl
from jax.experimental.pallas import tpu as pltpu
from jax.sharding import PartitionSpec as P

MESH = pl.DeviceIdType.MESH
REACH = 4
XS, YS, ZS = 4, 2, 8
GROUP = 2 * YS
MET = 2 * REACH + 1
EXTRA = 16
CHUNKS = 2
COPIES = 2 + 2 * (7 * CHUNKS + 1) + MET + 2 * REACH + 3 + 12 + 4 * (XS - 1) + 4 * (ZS - 1)
PARTS = 32000.0
LAST = (((1,), (1,)), ((), ()))
FIRST = (((0,), (0,)), ((), ()))
F32, BF16 = jnp.float32, jnp.bfloat16


def column_order():
    order = np.arange(XS * YS * ZS * 2 * 12).reshape(XS, YS, ZS, 2, 12)
    return order.transpose(1, 3, 0, 2, 4).reshape(1, -1).astype(np.int32)


def as_row(column):
    n = column.shape[0]
    return jnp.transpose(jnp.broadcast_to(column, (n, n)))[:8]


def as_column(row):
    n = row.shape[1]
    return jnp.transpose(jnp.broadcast_to(row, (n, n)))[:, :1]


def kernel(
    picture_hbm, caption_hbm, picture_head_hbm, caption_head_hbm, match_ref, scale_ref, offset_ref, order_ref,
    loss_out, image_out, text_out,
    picture_ref, caption_ref, picture_head, caption_head, raws, norm_out, norm_in, texts, images, part_own, part_out, part_in, slope_out, slope_in,
    loss_sum, dot_sum, towers_out, towers, backs, total, x_out, x_in, z_own, z_out, z_in, load, send, recv,
):
    dp, side = lax.axis_index("dp"), lax.axis_index("head")
    core = lax.rem(dp, 2)
    z = lax.rem(lax.div(dp, 2), ZS)
    y = lax.rem(lax.div(dp, 2 * ZS), YS)
    x = lax.div(dp, 2 * ZS * YS)
    blocks = XS * YS * ZS * 2
    rows, columns = picture_ref.shape
    half = picture_head.shape[1]

    loads = [
        pltpu.make_async_copy(caption_hbm, caption_ref, load.at[0]),
        pltpu.make_async_copy(caption_head_hbm, caption_head, load.at[1]),
        pltpu.make_async_copy(picture_hbm, picture_ref, load.at[2]),
        pltpu.make_async_copy(picture_head_hbm, picture_head, load.at[3]),
    ]
    for copy_in in loads:
        copy_in.start()

    def place(x, y, z, core):
        return ((x * YS + y) * ZS + z) * 2 + core

    def block(by):
        return (lax.rem(dp + by + blocks, blocks), side)

    peer = (dp, 1 - side)
    sibling = (dp + 1 - 2 * core, side)
    over = (place(x, 1 - y, z, core), side)
    crossed = [(place(x, 1 - y, z, c), 1 - side) for c in range(2)]
    x_peers = [(place(lax.rem(x + d, XS), y, z, core), side) for d in range(1, XS)]
    z_peers = [(place(x, y, lax.rem(z + d, ZS), core), side) for d in range(1, ZS)]
    near = [block(by) for by in range(-REACH, REACH + 1) if by]
    greeted = [peer, over, *crossed, *near, *x_peers, *z_peers]
    barrier = pltpu.get_barrier_semaphore()
    for other in greeted:
        pl.semaphore_signal(barrier, inc=1, device_id=other, device_id_type=MESH)

    mine = y * 2 + core
    cross_slot = (1 - y) * 2
    part = columns // GROUP
    wide = columns // XS
    cut = half // 2
    used = [0]
    sent = []

    def copy(src, dst, target, arrival=None):
        at = used[0]
        used[0] += 1
        at_arrival = at if arrival is None else arrival
        made = pltpu.make_async_remote_copy(
            src_ref=src, dst_ref=dst, send_sem=send.at[at], recv_sem=recv.at[at_arrival],
            device_id=target, device_id_type=MESH,
        )
        made.start()
        sent.append(made)
        return at

    def landed(dst, at):
        pltpu.make_async_copy(dst, dst, recv.at[at]).wait()

    norm_at = []
    for t, tower_ref, head in ((0, caption_ref, caption_head), (1, picture_ref, picture_head)):
        loads[2 * t].wait()
        loads[2 * t + 1].wait()
        raw = jnp.dot(tower_ref[...], head[...], preferred_element_type=F32)
        raws[t] = raw
        norm_out[t] = as_row(jnp.sum(raw * raw, axis=1, keepdims=True))
        if t == 0:
            pl.semaphore_wait(barrier, len(greeted))
        norm_at.append(copy(norm_out.at[t], norm_in.at[t], peer))

    def embedding(t):
        landed(norm_in.at[t], norm_at[t])
        inverse = lax.rsqrt(as_column((norm_out[t] + norm_in[t])[:1]) + 1e-06)
        return (raws[t] * inverse).astype(BF16), inverse

    size = rows // CHUNKS

    def piece(held, slot, c):
        return held.at[slot, pl.ds(c * size, size)]

    def spread_own(held):
        at = {}
        for c in range(CHUNKS):
            for by in (2, -2):
                at[by, c] = copy(piece(held, REACH, c), piece(held, REACH - by, c), block(by))
        at["own"] = copy(held.at[REACH], held.at[REACH + 2 * core - 1], sibling)
        return at

    def relay(held, at):
        for c in range(CHUNKS):
            for by in (2, -2):
                landed(piece(held, REACH - by, c), at[by, c])
                at["on", by, c] = copy(piece(held, REACH - by, c), piece(held, REACH - 2 * by, c), block(by))
            for name, by in (("up", 2), ("down", -2)):
                hand_over(held, at, name, by, c)

    def relayed(held, at):
        for c in range(CHUNKS):
            for by in (2, -2):
                landed(piece(held, REACH - 2 * by, c), at["on", by, c])
            hand_over(held, at, "outer", outer, c)

    def hand_over(held, at, name, by, c):
        at[name, c] = copy(piece(held, REACH + by, c), piece(held, REACH + by - 1 + 2 * core, c), sibling)

    def handed(held, at, name):
        for c in range(CHUNKS):
            landed(piece(held, slot_of[name], c), at[name, c])

    outer = 4 - 8 * core
    slot_of = {
        "own": REACH + 1 - 2 * core,
        "up": REACH + 3 - 2 * core,
        "down": REACH - 1 - 2 * core,
        "outer": REACH - 3 + 6 * core,
    }

    pair = jnp.concatenate([picture_ref[...], caption_ref[...]], axis=0)
    for g in range(GROUP):
        pick = order_ref[:, g * part : (g + 1) * part]
        acc = None
        for b in range(XS):
            chosen = lax.broadcasted_iota(jnp.int32, (wide, part), 0) + b * wide == pick
            one = jnp.where(chosen, 1.0, 0.0).astype(BF16)
            term = jnp.dot(pair[:, b * wide : (b + 1) * wide], one, preferred_element_type=F32)
            acc = term if acc is None else acc + term
        towers_out[g, 0] = acc[:rows].astype(BF16)
        towers_out[g, 1] = acc[rows:].astype(BF16)
    towers[mine] = towers_out[mine]
    tower_at = copy(towers_out.at[y * 2 + 1 - core], towers.at[mine], sibling)
    cross_at = used[0]
    for c in range(2):
        copy(towers_out.at[cross_slot + c], towers.at[mine], crossed[c], cross_at + core)


    text_emb, text_inv = embedding(0)
    texts[REACH] = text_emb
    text_at = spread_own(texts)
    image_emb, image_inv = embedding(1)
    images[REACH] = image_emb

    part_at = {}

    def logits(key, slot):
        value = lax.dot_general(images[REACH], texts[slot], LAST, preferred_element_type=F32)
        part_own[slot] = value
        part_out[slot] = jnp.round(value * PARTS).astype(jnp.int32).astype(jnp.int16)
        part_at[key] = copy(part_out.at[slot], part_in.at[slot], peer)

    scale, offset = scale_ref[0], offset_ref[0]
    match = as_column(match_ref[...].astype(F32))
    positive = jnp.where(
        lax.broadcasted_iota(jnp.int32, (rows, rows), 1).astype(F32) == match, 1.0, 0.0
    )
    slope_at = {}

    def slopes(key, slot, by):
        landed(part_in.at[slot], part_at[key])
        other = part_in[slot].astype(jnp.int32).astype(F32) * (1.0 / PARTS)
        product = scale * (part_own[slot] + other)
        logit = product + offset
        small = jnp.exp(-jnp.abs(logit))
        inverse = 1.0 / (1.0 + small)
        sigmoid = jnp.where(logit >= 0.0, inverse, small * inverse)
        loss = jnp.maximum(logit, 0.0) + jnp.log1p(small)
        if key == 0:
            sigmoid = sigmoid - positive
            loss = loss - positive * logit
        slope = (sigmoid * (1.0 / rows)).astype(BF16)
        weighted = slope.astype(F32) * product
        if key == 0:
            loss_sum[...] = loss
            dot_sum[...] = weighted
        else:
            loss_sum[...] += loss
            dot_sum[...] += weighted
        over_images = jnp.sum(weighted, axis=0, keepdims=True)
        high = over_images.astype(BF16).astype(F32)
        middle = (over_images - high).astype(BF16).astype(F32)
        low = over_images - high - middle
        extra = jnp.concatenate([high, middle, low, jnp.zeros((EXTRA - 3, rows), F32)], axis=0)
        slope_out[slot, :rows] = slope
        slope_out[slot, rows:] = extra.astype(BF16)
        if key == 0:
            slope_in[REACH] = slope_out[REACH]
        else:
            slope_at[key] = copy(slope_out.at[slot], slope_in.at[2 * REACH - slot], block(by))

    logits(0, REACH)
    landed(texts.at[slot_of["own"]], text_at["own"])
    logits("own", slot_of["own"])
    relay(texts, text_at)
    image_at = spread_own(images)
    for by in (2, -2):
        logits(by, REACH + by)
    slopes(0, REACH, 0)
    slopes("own", slot_of["own"], 1 - 2 * core)
    for name in ("up", "down"):
        handed(texts, text_at, name)
        logits(name, slot_of[name])
    relayed(texts, text_at)
    for by in (4, -4):
        logits(by, REACH + by)
    handed(texts, text_at, "outer")
    logits("outer", slot_of["outer"])
    for by in (2, -2):
        slopes(by, REACH + by, by)
    for name in ("up", "down"):
        slopes(name, slot_of[name], slot_of[name] - REACH)
    for by in (4, -4):
        slopes(by, REACH + by, by)
    slopes("outer", slot_of["outer"], slot_of["outer"] - REACH)

    relay(images, image_at)
    def back_through(gradient, emb, dot, inverse):
        return ((scale * gradient - emb.astype(F32) * dot) * inverse).astype(BF16)

    across = jnp.concatenate([slope_out[k, :rows] for k in range(MET)], axis=1)
    gradient = jnp.dot(across, texts[...].reshape(MET * rows, half), preferred_element_type=F32)
    image_dot = jnp.sum(dot_sum[...], axis=1, keepdims=True)
    back = back_through(gradient, images[REACH], image_dot, image_inv)
    back_at = {}

    def spread_back(t, back):
        for h in range(2):
            backs[t, h, mine] = back[:, h * cut : (h + 1) * cut]
            back_at[t, h, "over"] = copy(backs.at[t, h, mine], backs.at[t, h, mine], over)
        for h in range(2):
            back_at[t, h, "sibling"] = copy(backs.at[t, h, mine], backs.at[t, h, mine], sibling)

    spread_back(0, back)
    loss_out[...] = as_row(jnp.sum(loss_sum[...], axis=1, keepdims=True))[:1] * (1.0 / rows)

    relayed(images, image_at)

    came = {-2: -2, 2: 2, -4: -4, 4: 4, "own": None, "up": None, "down": None, "outer": None}
    slope_slot = {
        "own": REACH + 1 - 2 * core,
        "up": REACH - 1 - 2 * core,
        "down": REACH + 3 - 2 * core,
        "outer": REACH - 3 + 6 * core,
    }
    for name in came:
        slot = REACH - name if came[name] else slope_slot[name]
        landed(slope_in.at[slot], slope_at[name])
    landed(images.at[slot_of["own"]], image_at["own"])
    for name in ("up", "down", "outer"):
        handed(images, image_at, name)
    text_dot = None
    for k in range(MET):
        rows3 = jnp.sum(slope_in[k, rows:].astype(F32), axis=0, keepdims=True)
        text_dot = rows3 if text_dot is None else text_dot + rows3
    down = jnp.concatenate([slope_in[k, :rows] for k in range(MET)], axis=0)
    gradient = lax.dot_general(
        down, images[...].reshape(MET * rows, half), FIRST, preferred_element_type=F32
    )
    spread_back(1, back_through(gradient, texts[REACH], as_column(text_dot), text_inv))

    far = cross_slot + core
    landed(towers.at[y * 2 + 1 - core], tower_at)
    for c in range(2):
        landed(towers.at[cross_slot + c], cross_at + c)
    x_at = {}
    parts = [(t, h) for t in range(2) for h in range(2)]
    for t, h in parts:
        held = backs.at[t, h]
        landed(held.at[far], back_at[t, h, "over"])
        passed = copy(held.at[far], held.at[far], sibling)
        landed(held.at[y * 2 + 1 - core], back_at[t, h, "sibling"])
        landed(held.at[cross_slot + 1 - core], passed)
        product = lax.dot_general(
            towers[:, t].reshape(GROUP * rows, part), backs[t, h].reshape(GROUP * rows, cut),
            FIRST, preferred_element_type=F32,
        ).reshape(XS, part // XS, cut)
        total[t, h] = product
        x_out[t, h] = product.astype(BF16)
        for d in range(1, XS):
            x_at[t, h, d] = copy(x_out.at[t, h, lax.rem(x + d, XS)], x_in.at[t, h, d - 1], x_peers[d - 1])
    z_at = {}
    for t, h in parts:
        value = total[t, h, x]
        for d in range(1, XS):
            landed(x_in.at[t, h, d - 1], x_at[t, h, d])
            value = value + x_in[t, h, d - 1].astype(F32)
        for c in range(ZS):
            chunk = value[c * 12 : (c + 1) * 12]
            chunk = jnp.concatenate([chunk, jnp.zeros((4, cut), F32)], axis=0)
            z_own[t, h, c] = chunk
            z_out[t, h, c] = chunk.astype(BF16)
        for d in range(1, ZS):
            z_at[t, h, d] = copy(z_out.at[t, h, lax.rem(z + d, ZS)], z_in.at[t, h, d - 1], z_peers[d - 1])
    for t, h in parts:
        value = z_own[t, h, z]
        for d in range(1, ZS):
            landed(z_in.at[t, h, d - 1], z_at[t, h, d])
            value = value + z_in[t, h, d - 1].astype(F32)
        (image_out, text_out)[t][:, h * cut : (h + 1) * cut] = value[:12]
    for made in sent:
        made.wait_send()


def results(loss_ref, image_ref, text_ref, loss_out, image_out, text_out):
    loss_out[...] = loss_ref[...]
    image_out[...] = image_ref[...]
    text_out[...] = text_ref[...]


def shards(
    picture_tower_summary,
    caption_tower_summary,
    picture_head_matrix,
    caption_head_matrix,
    matching_caption_row,
    affinity_scale,
    affinity_offset,
):
    rows, columns = picture_tower_summary.shape
    half = picture_head_matrix.shape[1]
    part = columns // GROUP
    vmem = pl.BlockSpec(memory_space=pltpu.VMEM)
    smem = pl.BlockSpec(memory_space=pltpu.SMEM)
    hbm = pl.BlockSpec(memory_space=pl.ANY)
    loss, image_grad_w, text_grad_w = pl.pallas_call(
        kernel,
        out_shape=[
            jax.ShapeDtypeStruct((1, rows), F32),
            jax.ShapeDtypeStruct((12, half), F32),
            jax.ShapeDtypeStruct((12, half), F32),
        ],
        in_specs=[hbm, hbm, hbm, hbm, vmem, smem, smem, vmem],
        out_specs=[vmem] * 3,
        scratch_shapes=[
            pltpu.VMEM((rows, columns), BF16),
            pltpu.VMEM((rows, columns), BF16),
            pltpu.VMEM((columns, half), BF16),
            pltpu.VMEM((columns, half), BF16),
            pltpu.VMEM((2, rows, half), F32),
            pltpu.VMEM((2, 8, rows), F32),
            pltpu.VMEM((2, 8, rows), F32),
            pltpu.VMEM((MET, rows, half), BF16),
            pltpu.VMEM((MET, rows, half), BF16),
            pltpu.VMEM((MET, rows, rows), F32),
            pltpu.VMEM((MET, rows, rows), jnp.int16),
            pltpu.VMEM((MET, rows, rows), jnp.int16),
            pltpu.VMEM((MET, rows + EXTRA, rows), BF16),
            pltpu.VMEM((MET, rows + EXTRA, rows), BF16),
            pltpu.VMEM((rows, rows), F32),
            pltpu.VMEM((rows, rows), F32),
            pltpu.VMEM((GROUP, 2, rows, part), BF16),
            pltpu.VMEM((GROUP, 2, rows, part), BF16),
            pltpu.VMEM((2, 2, GROUP, rows, half // 2), BF16),
            pltpu.VMEM((2, 2, XS, part // XS, half // 2), F32),
            pltpu.VMEM((2, 2, XS, part // XS, half // 2), BF16),
            pltpu.VMEM((2, 2, XS - 1, part // XS, half // 2), BF16),
            pltpu.VMEM((2, 2, ZS, 16, half // 2), F32),
            pltpu.VMEM((2, 2, ZS, 16, half // 2), BF16),
            pltpu.VMEM((2, 2, ZS - 1, 16, half // 2), BF16),
            pltpu.SemaphoreType.DMA((4,)),
            pltpu.SemaphoreType.DMA((COPIES,)),
            pltpu.SemaphoreType.DMA((COPIES,)),
        ],
        compiler_params=pltpu.CompilerParams(
            collective_id=0, has_side_effects=True, vmem_limit_bytes=56 * 1024 * 1024
        ),
    )(
        picture_tower_summary, caption_tower_summary, picture_head_matrix, caption_head_matrix,
        matching_caption_row, affinity_scale, affinity_offset, jnp.asarray(column_order()),
    )
    loss, image_grad_w, text_grad_w = pl.pallas_call(
        results,
        out_shape=[
            jax.ShapeDtypeStruct((1, rows), F32),
            jax.ShapeDtypeStruct((12, half), F32),
            jax.ShapeDtypeStruct((12, half), F32),
        ],
        in_specs=[vmem] * 3,
        out_specs=[vmem] * 3,
    )(loss, image_grad_w, text_grad_w)
    return loss[0], image_grad_w, text_grad_w


def solution(mesh):
    return jax.shard_map(
        shards,
        mesh=mesh,
        in_specs=(
            P("dp", None),
            P("dp", None),
            P(None, "head"),
            P(None, "head"),
            P("dp", None),
            P(),
            P(),
        ),
        out_specs=(P("dp"), P("dp", "head"), P("dp", "head")),
        check_vma=False,
    )
```

```python
import jax
import jax.numpy as jnp
import numpy as np
from jax import lax
from jax.experimental import pallas as pl
from jax.experimental.pallas import tpu as pltpu
from jax.sharding import PartitionSpec as P

MESH = pl.DeviceIdType.MESH
REACH = 4
XS, YS, ZS = 4, 2, 8
GROUP = 2 * YS
MET = 2 * REACH + 1
EXTRA = 16
CHUNKS = 2
COPIES = 2 + 2 * (7 * CHUNKS + 1) + MET + 2 * REACH + 3 + 12 + 4 * (XS - 1) + 4 * (ZS - 1)
PARTS = 32000.0
LAST = (((1,), (1,)), ((), ()))
FIRST = (((0,), (0,)), ((), ()))
F32, BF16 = jnp.float32, jnp.bfloat16


def column_order():
    order = np.arange(XS * YS * ZS * 2 * 12).reshape(XS, YS, ZS, 2, 12)
    return order.transpose(1, 3, 0, 2, 4).reshape(1, -1).astype(np.int32)


def as_row(column):
    n = column.shape[0]
    return jnp.transpose(jnp.broadcast_to(column, (n, n)))[:8]


def as_column(row):
    n = row.shape[1]
    return jnp.transpose(jnp.broadcast_to(row, (n, n)))[:, :1]


def kernel(
    picture_hbm, caption_hbm, picture_head_hbm, caption_head_hbm, match_ref, scale_ref, offset_ref, order_ref,
    loss_out, image_out, text_out,
    picture_ref, caption_ref, picture_head, caption_head, raws, norm_out, norm_in, texts, images, part_own, part_out, part_in, slope_out, slope_in,
    loss_sum, dot_sum, towers_out, towers, backs, total, x_out, x_in, z_own, z_out, z_in, load, send, recv,
):
    dp, side = lax.axis_index("dp"), lax.axis_index("head")
    core = lax.rem(dp, 2)
    z = lax.rem(lax.div(dp, 2), ZS)
    y = lax.rem(lax.div(dp, 2 * ZS), YS)
    x = lax.div(dp, 2 * ZS * YS)
    blocks = XS * YS * ZS * 2
    rows, columns = picture_ref.shape
    half = picture_head.shape[1]

    loads = [
        pltpu.make_async_copy(caption_hbm, caption_ref, load.at[0]),
        pltpu.make_async_copy(picture_hbm, picture_ref, load.at[1]),
        pltpu.make_async_copy(caption_head_hbm, caption_head, load.at[2]),
        pltpu.make_async_copy(picture_head_hbm, picture_head, load.at[3]),
    ]
    for copy_in in loads:
        copy_in.start()

    def place(x, y, z, core):
        return ((x * YS + y) * ZS + z) * 2 + core

    def block(by):
        return (lax.rem(dp + by + blocks, blocks), side)

    peer = (dp, 1 - side)
    sibling = (dp + 1 - 2 * core, side)
    over = (place(x, 1 - y, z, core), side)
    crossed = [(place(x, 1 - y, z, c), 1 - side) for c in range(2)]
    x_peers = [(place(lax.rem(x + d, XS), y, z, core), side) for d in range(1, XS)]
    z_peers = [(place(x, y, lax.rem(z + d, ZS), core), side) for d in range(1, ZS)]
    near = [block(by) for by in range(-REACH, REACH + 1) if by]
    greeted = [peer, over, *crossed, *near, *x_peers, *z_peers]
    barrier = pltpu.get_barrier_semaphore()
    for other in greeted:
        pl.semaphore_signal(barrier, inc=1, device_id=other, device_id_type=MESH)

    mine = y * 2 + core
    cross_slot = (1 - y) * 2
    part = columns // GROUP
    wide = columns // XS
    cut = half // 2
    used = [0]
    sent = []

    def copy(src, dst, target, arrival=None):
        at = used[0]
        used[0] += 1
        at_arrival = at if arrival is None else arrival
        made = pltpu.make_async_remote_copy(
            src_ref=src, dst_ref=dst, send_sem=send.at[at], recv_sem=recv.at[at_arrival],
            device_id=target, device_id_type=MESH,
        )
        made.start()
        sent.append(made)
        return at

    def settle(count):
        for made in sent[:count]:
            made.wait_send()
        del sent[:count]

    def landed(dst, at):
        pltpu.make_async_copy(dst, dst, recv.at[at]).wait()

    loads[0].wait()
    loads[1].wait()
    norm_at = []
    for t, tower_ref, head in ((0, caption_ref, caption_head), (1, picture_ref, picture_head)):
        loads[2 + t].wait()
        raw = jnp.dot(tower_ref[...], head[...], preferred_element_type=F32)
        raws[t] = raw
        norm_out[t] = as_row(jnp.sum(raw * raw, axis=1, keepdims=True))
        if t == 0:
            pl.semaphore_wait(barrier, len(greeted))
        norm_at.append(copy(norm_out.at[t], norm_in.at[t], peer))
        if t == 0:
            pair = jnp.concatenate([picture_ref[...], caption_ref[...]], axis=0)
            lane = lax.broadcasted_iota(jnp.int32, (1, part), 1)
            step = part // XS
            section = sum(jnp.where(lane >= b * step, 1, 0) for b in range(1, XS))
            for g in range(GROUP):
                pick = order_ref[:, g * part : (g + 1) * part] - section * wide
                chosen = lax.broadcasted_iota(jnp.int32, (wide, part), 0) == pick
                one = jnp.where(chosen, 1.0, 0.0).astype(BF16)
                acc = None
                for b in range(XS):
                    term = jnp.dot(pair[:, b * wide : (b + 1) * wide], one, preferred_element_type=F32)
                    acc = term if acc is None else jnp.where(section == b, term, acc)
                towers_out[g, 0] = acc[:rows].astype(BF16)
                towers_out[g, 1] = acc[rows:].astype(BF16)
            towers[mine] = towers_out[mine]
            tower_at = copy(towers_out.at[y * 2 + 1 - core], towers.at[mine], sibling)
            cross_at = used[0]
            for c in range(2):
                copy(towers_out.at[cross_slot + c], towers.at[mine], crossed[c], cross_at + core)

    def embedding(t):
        landed(norm_in.at[t], norm_at[t])
        inverse = lax.rsqrt(as_column((norm_out[t] + norm_in[t])[:1]) + 1e-06)
        return (raws[t] * inverse).astype(BF16), inverse

    size = rows // CHUNKS

    def piece(held, slot, c):
        return held.at[slot, pl.ds(c * size, size)]

    def spread_own(held):
        at = {}
        for c in range(CHUNKS):
            for by in (2, -2):
                at[by, c] = copy(piece(held, REACH, c), piece(held, REACH - by, c), block(by))
        at["own"] = copy(held.at[REACH], held.at[REACH + 2 * core - 1], sibling)
        return at

    def relay(held, at):
        for c in range(CHUNKS):
            for by in (2, -2):
                landed(piece(held, REACH - by, c), at[by, c])
                at["on", by, c] = copy(piece(held, REACH - by, c), piece(held, REACH - 2 * by, c), block(by))
            for name, by in (("up", 2), ("down", -2)):
                hand_over(held, at, name, by, c)

    def relayed(held, at):
        for c in range(CHUNKS):
            for by in (2, -2):
                landed(piece(held, REACH - 2 * by, c), at["on", by, c])
            hand_over(held, at, "outer", outer, c)

    def hand_over(held, at, name, by, c):
        at[name, c] = copy(piece(held, REACH + by, c), piece(held, REACH + by - 1 + 2 * core, c), sibling)

    def handed(held, at, name):
        for c in range(CHUNKS):
            landed(piece(held, slot_of[name], c), at[name, c])

    outer = 4 - 8 * core
    slot_of = {
        "own": REACH + 1 - 2 * core,
        "up": REACH + 3 - 2 * core,
        "down": REACH - 1 - 2 * core,
        "outer": REACH - 3 + 6 * core,
    }

    text_emb, text_inv = embedding(0)
    texts[REACH] = text_emb
    text_at = spread_own(texts)
    image_emb, image_inv = embedding(1)
    images[REACH] = image_emb

    part_at = {}

    def logits(key, slot):
        value = lax.dot_general(images[REACH], texts[slot], LAST, preferred_element_type=F32)
        part_own[slot] = value
        part_out[slot] = jnp.round(value * PARTS).astype(jnp.int32).astype(jnp.int16)
        part_at[key] = copy(part_out.at[slot], part_in.at[slot], peer)

    scale, offset = scale_ref[0], offset_ref[0]
    match = as_column(match_ref[...].astype(F32))
    positive = jnp.where(
        lax.broadcasted_iota(jnp.int32, (rows, rows), 1).astype(F32) == match, 1.0, 0.0
    )
    slope_at = {}

    def slopes(key, slot, by):
        landed(part_in.at[slot], part_at[key])
        other = part_in[slot].astype(jnp.int32).astype(F32) * (1.0 / PARTS)
        product = scale * (part_own[slot] + other)
        logit = product + offset
        small = jnp.exp(-jnp.abs(logit))
        inverse = 1.0 / (1.0 + small)
        sigmoid = jnp.where(logit >= 0.0, inverse, small * inverse)
        loss = jnp.maximum(logit, 0.0) + jnp.log1p(small)
        if key == 0:
            sigmoid = sigmoid - positive
            loss = loss - positive * logit
        slope = (sigmoid * (1.0 / rows)).astype(BF16)
        weighted = slope.astype(F32) * product
        if key == 0:
            loss_sum[...] = loss
            dot_sum[...] = weighted
        else:
            loss_sum[...] += loss
            dot_sum[...] += weighted
        over_images = jnp.sum(weighted, axis=0, keepdims=True)
        high = over_images.astype(BF16).astype(F32)
        middle = (over_images - high).astype(BF16).astype(F32)
        low = over_images - high - middle
        extra = jnp.concatenate([high, middle, low, jnp.zeros((EXTRA - 3, rows), F32)], axis=0)
        slope_out[slot, :rows] = slope
        slope_out[slot, rows:] = extra.astype(BF16)
        if key == 0:
            slope_in[REACH] = slope_out[REACH]
        else:
            slope_at[key] = copy(slope_out.at[slot], slope_in.at[2 * REACH - slot], block(by))

    logits(0, REACH)
    landed(texts.at[slot_of["own"]], text_at["own"])
    logits("own", slot_of["own"])
    relay(texts, text_at)
    image_at = spread_own(images)
    for by in (2, -2):
        logits(by, REACH + by)
    slopes(0, REACH, 0)
    slopes("own", slot_of["own"], 1 - 2 * core)
    for name in ("up", "down"):
        handed(texts, text_at, name)
        logits(name, slot_of[name])
    relayed(texts, text_at)
    for by in (4, -4):
        logits(by, REACH + by)
    handed(texts, text_at, "outer")
    logits("outer", slot_of["outer"])
    for by in (2, -2):
        slopes(by, REACH + by, by)
    for name in ("up", "down"):
        slopes(name, slot_of[name], slot_of[name] - REACH)
    for by in (4, -4):
        slopes(by, REACH + by, by)
    slopes("outer", slot_of["outer"], slot_of["outer"] - REACH)

    relay(images, image_at)
    def back_through(gradient, emb, dot, inverse):
        return ((scale * gradient - emb.astype(F32) * dot) * inverse).astype(BF16)

    across = jnp.concatenate([slope_out[k, :rows] for k in range(MET)], axis=1)
    gradient = jnp.dot(across, texts[...].reshape(MET * rows, half), preferred_element_type=F32)
    image_dot = jnp.sum(dot_sum[...], axis=1, keepdims=True)
    back = back_through(gradient, images[REACH], image_dot, image_inv)
    back_at = {}

    def spread_back(t, back):
        for h in range(2):
            backs[t, h, mine] = back[:, h * cut : (h + 1) * cut]
            back_at[t, h, "over"] = copy(backs.at[t, h, mine], backs.at[t, h, mine], over)
        for h in range(2):
            back_at[t, h, "sibling"] = copy(backs.at[t, h, mine], backs.at[t, h, mine], sibling)

    early = len(sent)
    spread_back(0, back)
    loss_out[...] = as_row(jnp.sum(loss_sum[...], axis=1, keepdims=True))[:1] * (1.0 / rows)

    relayed(images, image_at)

    came = {-2: -2, 2: 2, -4: -4, 4: 4, "own": None, "up": None, "down": None, "outer": None}
    slope_slot = {
        "own": REACH + 1 - 2 * core,
        "up": REACH - 1 - 2 * core,
        "down": REACH + 3 - 2 * core,
        "outer": REACH - 3 + 6 * core,
    }
    for name in came:
        slot = REACH - name if came[name] else slope_slot[name]
        landed(slope_in.at[slot], slope_at[name])
    landed(images.at[slot_of["own"]], image_at["own"])
    for name in ("up", "down", "outer"):
        handed(images, image_at, name)
    text_dot = None
    for k in range(MET):
        rows3 = jnp.sum(slope_in[k, rows:].astype(F32), axis=0, keepdims=True)
        text_dot = rows3 if text_dot is None else text_dot + rows3
    down = jnp.concatenate([slope_in[k, :rows] for k in range(MET)], axis=0)
    gradient = lax.dot_general(
        down, images[...].reshape(MET * rows, half), FIRST, preferred_element_type=F32
    )
    spread_back(1, back_through(gradient, texts[REACH], as_column(text_dot), text_inv))
    settle(early)

    far = cross_slot + core
    landed(towers.at[y * 2 + 1 - core], tower_at)
    for c in range(2):
        landed(towers.at[cross_slot + c], cross_at + c)
    x_at = {}
    parts = [(t, h) for t in range(2) for h in range(2)]
    for t, h in parts:
        held = backs.at[t, h]
        landed(held.at[far], back_at[t, h, "over"])
        passed = copy(held.at[far], held.at[far], sibling)
        landed(held.at[y * 2 + 1 - core], back_at[t, h, "sibling"])
        landed(held.at[cross_slot + 1 - core], passed)
        product = lax.dot_general(
            towers[:, t].reshape(GROUP * rows, part), backs[t, h].reshape(GROUP * rows, cut),
            FIRST, preferred_element_type=F32,
        ).reshape(XS, part // XS, cut)
        total[t, h] = product
        x_out[t, h] = product.astype(BF16)
        for d in range(1, XS):
            x_at[t, h, d] = copy(x_out.at[t, h, lax.rem(x + d, XS)], x_in.at[t, h, d - 1], x_peers[d - 1])
    settle(len(sent) - 2 * 2 * (XS - 1) // 2)
    z_at = {}
    for t, h in parts:
        value = total[t, h, x]
        for d in range(1, XS):
            landed(x_in.at[t, h, d - 1], x_at[t, h, d])
            value = value + x_in[t, h, d - 1].astype(F32)
        for c in range(ZS):
            chunk = value[c * 12 : (c + 1) * 12]
            chunk = jnp.concatenate([chunk, jnp.zeros((4, cut), F32)], axis=0)
            z_own[t, h, c] = chunk
            z_out[t, h, c] = chunk.astype(BF16)
        for d in range(1, ZS):
            z_at[t, h, d] = copy(z_out.at[t, h, lax.rem(z + d, ZS)], z_in.at[t, h, d - 1], z_peers[d - 1])
    settle(len(sent) - 4 * (ZS - 1))
    for t, h in parts:
        value = z_own[t, h, z]
        for d in range(1, ZS):
            landed(z_in.at[t, h, d - 1], z_at[t, h, d])
            value = value + z_in[t, h, d - 1].astype(F32)
        (image_out, text_out)[t][:, h * cut : (h + 1) * cut] = value[:12]
    settle(len(sent))


def results(loss_ref, image_ref, text_ref, loss_out, image_out, text_out):
    loss_out[...] = loss_ref[...]
    image_out[...] = image_ref[...]
    text_out[...] = text_ref[...]


def shards(
    picture_tower_summary,
    caption_tower_summary,
    picture_head_matrix,
    caption_head_matrix,
    matching_caption_row,
    affinity_scale,
    affinity_offset,
):
    rows, columns = picture_tower_summary.shape
    half = picture_head_matrix.shape[1]
    part = columns // GROUP
    vmem = pl.BlockSpec(memory_space=pltpu.VMEM)
    smem = pl.BlockSpec(memory_space=pltpu.SMEM)
    hbm = pl.BlockSpec(memory_space=pl.ANY)
    loss, image_grad_w, text_grad_w = pl.pallas_call(
        kernel,
        out_shape=[
            jax.ShapeDtypeStruct((1, rows), F32),
            jax.ShapeDtypeStruct((12, half), F32),
            jax.ShapeDtypeStruct((12, half), F32),
        ],
        in_specs=[hbm, hbm, hbm, hbm, vmem, smem, smem, vmem],
        out_specs=[vmem] * 3,
        scratch_shapes=[
            pltpu.VMEM((rows, columns), BF16),
            pltpu.VMEM((rows, columns), BF16),
            pltpu.VMEM((columns, half), BF16),
            pltpu.VMEM((columns, half), BF16),
            pltpu.VMEM((2, rows, half), F32),
            pltpu.VMEM((2, 8, rows), F32),
            pltpu.VMEM((2, 8, rows), F32),
            pltpu.VMEM((MET, rows, half), BF16),
            pltpu.VMEM((MET, rows, half), BF16),
            pltpu.VMEM((MET, rows, rows), F32),
            pltpu.VMEM((MET, rows, rows), jnp.int16),
            pltpu.VMEM((MET, rows, rows), jnp.int16),
            pltpu.VMEM((MET, rows + EXTRA, rows), BF16),
            pltpu.VMEM((MET, rows + EXTRA, rows), BF16),
            pltpu.VMEM((rows, rows), F32),
            pltpu.VMEM((rows, rows), F32),
            pltpu.VMEM((GROUP, 2, rows, part), BF16),
            pltpu.VMEM((GROUP, 2, rows, part), BF16),
            pltpu.VMEM((2, 2, GROUP, rows, half // 2), BF16),
            pltpu.VMEM((2, 2, XS, part // XS, half // 2), F32),
            pltpu.VMEM((2, 2, XS, part // XS, half // 2), BF16),
            pltpu.VMEM((2, 2, XS - 1, part // XS, half // 2), BF16),
            pltpu.VMEM((2, 2, ZS, 16, half // 2), F32),
            pltpu.VMEM((2, 2, ZS, 16, half // 2), BF16),
            pltpu.VMEM((2, 2, ZS - 1, 16, half // 2), BF16),
            pltpu.SemaphoreType.DMA((4,)),
            pltpu.SemaphoreType.DMA((COPIES,)),
            pltpu.SemaphoreType.DMA((COPIES,)),
        ],
        compiler_params=pltpu.CompilerParams(
            collective_id=0, has_side_effects=True, vmem_limit_bytes=56 * 1024 * 1024
        ),
    )(
        picture_tower_summary, caption_tower_summary, picture_head_matrix, caption_head_matrix,
        matching_caption_row, affinity_scale, affinity_offset, jnp.asarray(column_order()),
    )
    loss, image_grad_w, text_grad_w = pl.pallas_call(
        results,
        out_shape=[
            jax.ShapeDtypeStruct((1, rows), F32),
            jax.ShapeDtypeStruct((12, half), F32),
            jax.ShapeDtypeStruct((12, half), F32),
        ],
        in_specs=[vmem] * 3,
        out_specs=[vmem] * 3,
    )(loss, image_grad_w, text_grad_w)
    return loss[0], image_grad_w, text_grad_w


def solution(mesh):
    return jax.shard_map(
        shards,
        mesh=mesh,
        in_specs=(
            P("dp", None),
            P("dp", None),
            P(None, "head"),
            P(None, "head"),
            P("dp", None),
            P(),
            P(),
        ),
        out_specs=(P("dp"), P("dp", "head"), P("dp", "head")),
        check_vma=False,
    )
```

```python
import jax
import jax.numpy as jnp
import numpy as np
from jax import lax
from jax.experimental import pallas as pl
from jax.experimental.pallas import tpu as pltpu
from jax.sharding import PartitionSpec as P

MESH = pl.DeviceIdType.MESH
REACH = 4
XS, YS, ZS = 4, 2, 8
GROUP = 2 * YS
MET = 2 * REACH + 1
EXTRA = 16
CHUNKS = 2
COPIES = 2 + 2 * (7 * CHUNKS + 1) + MET + 2 * REACH + 3 + 12 + 4 * (XS - 1) + 4 * (ZS - 1)
PARTS = 32000.0
LAST = (((1,), (1,)), ((), ()))
FIRST = (((0,), (0,)), ((), ()))
F32, BF16 = jnp.float32, jnp.bfloat16


def column_order():
    order = np.arange(XS * YS * ZS * 2 * 12).reshape(XS, YS, ZS, 2, 12)
    return order.transpose(1, 3, 0, 2, 4).reshape(1, -1).astype(np.int32)


def as_row(column):
    n = column.shape[0]
    return jnp.transpose(jnp.broadcast_to(column, (n, n)))[:8]


def as_column(row):
    n = row.shape[1]
    return jnp.transpose(jnp.broadcast_to(row, (n, n)))[:, :1]


def kernel(
    picture_hbm, caption_hbm, picture_head_hbm, caption_head_hbm, match_ref, scale_ref, offset_ref, order_ref,
    loss_out, image_out, text_out,
    picture_ref, caption_ref, picture_head, caption_head, raws, norm_out, norm_in, texts, images, part_own, part_out, part_in, slope_out, slope_in,
    loss_sum, dot_sum, towers_out, towers, backs, total, x_out, x_in, z_own, z_out, z_in, load, send, recv,
):
    dp, side = lax.axis_index("dp"), lax.axis_index("head")
    core = lax.rem(dp, 2)
    z = lax.rem(lax.div(dp, 2), ZS)
    y = lax.rem(lax.div(dp, 2 * ZS), YS)
    x = lax.div(dp, 2 * ZS * YS)
    blocks = XS * YS * ZS * 2
    rows, columns = picture_ref.shape
    half = picture_head.shape[1]

    loads = [
        pltpu.make_async_copy(caption_hbm, caption_ref, load.at[0]),
        pltpu.make_async_copy(picture_hbm, picture_ref, load.at[1]),
        pltpu.make_async_copy(caption_head_hbm, caption_head, load.at[2]),
        pltpu.make_async_copy(picture_head_hbm, picture_head, load.at[3]),
    ]
    for copy_in in loads:
        copy_in.start()

    def place(x, y, z, core):
        return ((x * YS + y) * ZS + z) * 2 + core

    def block(by):
        return (lax.rem(dp + by + blocks, blocks), side)

    peer = (dp, 1 - side)
    sibling = (dp + 1 - 2 * core, side)
    over = (place(x, 1 - y, z, core), side)
    crossed = [(place(x, 1 - y, z, c), 1 - side) for c in range(2)]
    x_peers = [(place(lax.rem(x + d, XS), y, z, core), side) for d in range(1, XS)]
    z_peers = [(place(x, y, lax.rem(z + d, ZS), core), side) for d in range(1, ZS)]
    near = [block(by) for by in range(-REACH, REACH + 1) if by]
    greeted = [peer, over, *crossed, *near, *x_peers, *z_peers]
    barrier = pltpu.get_barrier_semaphore()
    for other in greeted:
        pl.semaphore_signal(barrier, inc=1, device_id=other, device_id_type=MESH)

    mine = y * 2 + core
    cross_slot = (1 - y) * 2
    part = columns // GROUP
    wide = columns // XS
    cut = half // 2
    used = [0]
    sent = []

    def copy(src, dst, target, arrival=None):
        at = used[0]
        used[0] += 1
        at_arrival = at if arrival is None else arrival
        made = pltpu.make_async_remote_copy(
            src_ref=src, dst_ref=dst, send_sem=send.at[at], recv_sem=recv.at[at_arrival],
            device_id=target, device_id_type=MESH,
        )
        made.start()
        sent.append(made)
        return at

    def settle(count):
        for made in sent[:count]:
            made.wait_send()
        del sent[:count]

    def landed(dst, at):
        pltpu.make_async_copy(dst, dst, recv.at[at]).wait()

    loads[0].wait()
    loads[1].wait()
    norm_at = []
    for t, tower_ref, head in ((0, caption_ref, caption_head), (1, picture_ref, picture_head)):
        loads[2 + t].wait()
        raw = jnp.dot(tower_ref[...], head[...], preferred_element_type=F32)
        raws[t] = raw
        norm_out[t] = as_row(jnp.sum(raw * raw, axis=1, keepdims=True))
        if t == 0:
            pl.semaphore_wait(barrier, len(greeted))
        norm_at.append(copy(norm_out.at[t], norm_in.at[t], peer))
        if t == 0:
            pair = jnp.concatenate([picture_ref[...], caption_ref[...]], axis=0)
            lane = lax.broadcasted_iota(jnp.int32, (1, part), 1)
            step = part // XS
            section = sum(jnp.where(lane >= b * step, 1, 0) for b in range(1, XS))
            for g in range(GROUP):
                pick = order_ref[:, g * part : (g + 1) * part] - section * wide
                chosen = lax.broadcasted_iota(jnp.int32, (wide, part), 0) == pick
                one = jnp.where(chosen, 1.0, 0.0).astype(BF16)
                acc = None
                for b in range(XS):
                    term = jnp.dot(pair[:, b * wide : (b + 1) * wide], one, preferred_element_type=F32)
                    acc = term if acc is None else jnp.where(section == b, term, acc)
                towers_out[g, 0] = acc[:rows].astype(BF16)
                towers_out[g, 1] = acc[rows:].astype(BF16)
            towers[mine] = towers_out[mine]
            tower_at = copy(towers_out.at[y * 2 + 1 - core], towers.at[mine], sibling)
            cross_at = used[0]
            for c in range(2):
                copy(towers_out.at[cross_slot + c], towers.at[mine], crossed[c], cross_at + core)

    def embedding(t):
        landed(norm_in.at[t], norm_at[t])
        inverse = lax.rsqrt(as_column((norm_out[t] + norm_in[t])[:1]) + 1e-06)
        return (raws[t] * inverse).astype(BF16), inverse

    def chunks(held):
        return CHUNKS if held is texts else 1

    def piece(held, slot, c):
        size = rows // chunks(held)
        return held.at[slot, pl.ds(c * size, size)]

    def spread_own(held):
        at = {}
        for c in range(chunks(held)):
            for by in (2, -2):
                at[by, c] = copy(piece(held, REACH, c), piece(held, REACH - by, c), block(by))
        at["own"] = copy(held.at[REACH], held.at[REACH + 2 * core - 1], sibling)
        return at

    def relay(held, at):
        for c in range(chunks(held)):
            for by in (2, -2):
                landed(piece(held, REACH - by, c), at[by, c])
                at["on", by, c] = copy(piece(held, REACH - by, c), piece(held, REACH - 2 * by, c), block(by))
            for name, by in (("up", 2), ("down", -2)):
                hand_over(held, at, name, by, c)

    def relayed(held, at):
        for c in range(chunks(held)):
            for by in (2, -2):
                landed(piece(held, REACH - 2 * by, c), at["on", by, c])
            hand_over(held, at, "outer", outer, c)

    def hand_over(held, at, name, by, c):
        at[name, c] = copy(piece(held, REACH + by, c), piece(held, REACH + by - 1 + 2 * core, c), sibling)

    def handed(held, at, name):
        for c in range(chunks(held)):
            landed(piece(held, slot_of[name], c), at[name, c])

    outer = 4 - 8 * core
    slot_of = {
        "own": REACH + 1 - 2 * core,
        "up": REACH + 3 - 2 * core,
        "down": REACH - 1 - 2 * core,
        "outer": REACH - 3 + 6 * core,
    }

    text_emb, text_inv = embedding(0)
    texts[REACH] = text_emb
    text_at = spread_own(texts)
    image_emb, image_inv = embedding(1)
    images[REACH] = image_emb

    part_at = {}

    def logits(key, slot):
        value = lax.dot_general(images[REACH], texts[slot], LAST, preferred_element_type=F32)
        part_own[slot] = value
        part_out[slot] = jnp.round(value * PARTS).astype(jnp.int32).astype(jnp.int16)
        part_at[key] = copy(part_out.at[slot], part_in.at[slot], peer)

    scale, offset = scale_ref[0], offset_ref[0]
    match = as_column(match_ref[...].astype(F32))
    positive = jnp.where(
        lax.broadcasted_iota(jnp.int32, (rows, rows), 1).astype(F32) == match, 1.0, 0.0
    )
    slope_at = {}

    def slopes(key, slot, by):
        landed(part_in.at[slot], part_at[key])
        other = part_in[slot].astype(jnp.int32).astype(F32) * (1.0 / PARTS)
        product = scale * (part_own[slot] + other)
        logit = product + offset
        small = jnp.exp(-jnp.abs(logit))
        inverse = 1.0 / (1.0 + small)
        sigmoid = jnp.where(logit >= 0.0, inverse, small * inverse)
        loss = jnp.maximum(logit, 0.0) + jnp.log1p(small)
        if key == 0:
            sigmoid = sigmoid - positive
            loss = loss - positive * logit
        slope = (sigmoid * (1.0 / rows)).astype(BF16)
        weighted = slope.astype(F32) * product
        if key == 0:
            loss_sum[...] = loss
            dot_sum[...] = weighted
        else:
            loss_sum[...] += loss
            dot_sum[...] += weighted
        over_images = jnp.sum(weighted, axis=0, keepdims=True)
        high = over_images.astype(BF16).astype(F32)
        middle = (over_images - high).astype(BF16).astype(F32)
        low = over_images - high - middle
        extra = jnp.concatenate([high, middle, low, jnp.zeros((EXTRA - 3, rows), F32)], axis=0)
        slope_out[slot, :rows] = slope
        slope_out[slot, rows:] = extra.astype(BF16)
        if key == 0:
            slope_in[REACH] = slope_out[REACH]
        else:
            slope_at[key] = copy(slope_out.at[slot], slope_in.at[2 * REACH - slot], block(by))

    logits(0, REACH)
    landed(texts.at[slot_of["own"]], text_at["own"])
    logits("own", slot_of["own"])
    relay(texts, text_at)
    image_at = spread_own(images)
    for by in (2, -2):
        logits(by, REACH + by)
    slopes(0, REACH, 0)
    slopes("own", slot_of["own"], 1 - 2 * core)
    for name in ("up", "down"):
        handed(texts, text_at, name)
        logits(name, slot_of[name])
    relayed(texts, text_at)
    for by in (4, -4):
        logits(by, REACH + by)
    handed(texts, text_at, "outer")
    logits("outer", slot_of["outer"])
    for by in (2, -2):
        slopes(by, REACH + by, by)
    for name in ("up", "down"):
        slopes(name, slot_of[name], slot_of[name] - REACH)
    for by in (4, -4):
        slopes(by, REACH + by, by)
    slopes("outer", slot_of["outer"], slot_of["outer"] - REACH)

    relay(images, image_at)
    def back_through(gradient, emb, dot, inverse):
        return ((scale * gradient - emb.astype(F32) * dot) * inverse).astype(BF16)

    across = jnp.concatenate([slope_out[k, :rows] for k in range(MET)], axis=1)
    gradient = jnp.dot(across, texts[...].reshape(MET * rows, half), preferred_element_type=F32)
    image_dot = jnp.sum(dot_sum[...], axis=1, keepdims=True)
    back = back_through(gradient, images[REACH], image_dot, image_inv)
    back_at = {}

    def spread_back(t, back):
        for h in range(2):
            backs[t, h, mine] = back[:, h * cut : (h + 1) * cut]
            back_at[t, h, "over"] = copy(backs.at[t, h, mine], backs.at[t, h, mine], over)
        for h in range(2):
            back_at[t, h, "sibling"] = copy(backs.at[t, h, mine], backs.at[t, h, mine], sibling)

    early = len(sent)
    spread_back(0, back)
    loss_out[...] = as_row(jnp.sum(loss_sum[...], axis=1, keepdims=True))[:1] * (1.0 / rows)

    relayed(images, image_at)

    came = {-2: -2, 2: 2, -4: -4, 4: 4, "own": None, "up": None, "down": None, "outer": None}
    slope_slot = {
        "own": REACH + 1 - 2 * core,
        "up": REACH - 1 - 2 * core,
        "down": REACH + 3 - 2 * core,
        "outer": REACH - 3 + 6 * core,
    }
    for name in came:
        slot = REACH - name if came[name] else slope_slot[name]
        landed(slope_in.at[slot], slope_at[name])
    landed(images.at[slot_of["own"]], image_at["own"])
    for name in ("up", "down", "outer"):
        handed(images, image_at, name)
    text_dot = None
    for k in range(MET):
        rows3 = jnp.sum(slope_in[k, rows:].astype(F32), axis=0, keepdims=True)
        text_dot = rows3 if text_dot is None else text_dot + rows3
    down = jnp.concatenate([slope_in[k, :rows] for k in range(MET)], axis=0)
    gradient = lax.dot_general(
        down, images[...].reshape(MET * rows, half), FIRST, preferred_element_type=F32
    )
    spread_back(1, back_through(gradient, texts[REACH], as_column(text_dot), text_inv))
    settle(early)

    far = cross_slot + core
    landed(towers.at[y * 2 + 1 - core], tower_at)
    for c in range(2):
        landed(towers.at[cross_slot + c], cross_at + c)
    x_at = {}
    parts = [(t, h) for t in range(2) for h in range(2)]
    for t, h in parts:
        held = backs.at[t, h]
        landed(held.at[far], back_at[t, h, "over"])
        passed = copy(held.at[far], held.at[far], sibling)
        landed(held.at[y * 2 + 1 - core], back_at[t, h, "sibling"])
        landed(held.at[cross_slot + 1 - core], passed)
        product = lax.dot_general(
            towers[:, t].reshape(GROUP * rows, part), backs[t, h].reshape(GROUP * rows, cut),
            FIRST, preferred_element_type=F32,
        ).reshape(XS, part // XS, cut)
        total[t, h] = product
        x_out[t, h] = product.astype(BF16)
        for d in range(1, XS):
            x_at[t, h, d] = copy(x_out.at[t, h, lax.rem(x + d, XS)], x_in.at[t, h, d - 1], x_peers[d - 1])
    settle(len(sent) - 2 * 2 * (XS - 1) // 2)
    z_at = {}
    for t, h in parts:
        value = total[t, h, x]
        for d in range(1, XS):
            landed(x_in.at[t, h, d - 1], x_at[t, h, d])
            value = value + x_in[t, h, d - 1].astype(F32)
        for c in range(ZS):
            chunk = value[c * 12 : (c + 1) * 12]
            chunk = jnp.concatenate([chunk, jnp.zeros((4, cut), F32)], axis=0)
            z_own[t, h, c] = chunk
            z_out[t, h, c] = chunk.astype(BF16)
        for d in range(1, ZS):
            z_at[t, h, d] = copy(z_out.at[t, h, lax.rem(z + d, ZS)], z_in.at[t, h, d - 1], z_peers[d - 1])
    settle(len(sent) - 4 * (ZS - 1))
    for t, h in parts:
        value = z_own[t, h, z]
        for d in range(1, ZS):
            landed(z_in.at[t, h, d - 1], z_at[t, h, d])
            value = value + z_in[t, h, d - 1].astype(F32)
        (image_out, text_out)[t][:, h * cut : (h + 1) * cut] = value[:12]
    settle(len(sent))


def results(loss_ref, image_ref, text_ref, loss_out, image_out, text_out):
    loss_out[...] = loss_ref[...]
    image_out[...] = image_ref[...]
    text_out[...] = text_ref[...]


def shards(
    picture_tower_summary,
    caption_tower_summary,
    picture_head_matrix,
    caption_head_matrix,
    matching_caption_row,
    affinity_scale,
    affinity_offset,
):
    rows, columns = picture_tower_summary.shape
    half = picture_head_matrix.shape[1]
    part = columns // GROUP
    vmem = pl.BlockSpec(memory_space=pltpu.VMEM)
    smem = pl.BlockSpec(memory_space=pltpu.SMEM)
    hbm = pl.BlockSpec(memory_space=pl.ANY)
    loss, image_grad_w, text_grad_w = pl.pallas_call(
        kernel,
        out_shape=[
            jax.ShapeDtypeStruct((1, rows), F32),
            jax.ShapeDtypeStruct((12, half), F32),
            jax.ShapeDtypeStruct((12, half), F32),
        ],
        in_specs=[hbm, hbm, hbm, hbm, vmem, smem, smem, vmem],
        out_specs=[vmem] * 3,
        scratch_shapes=[
            pltpu.VMEM((rows, columns), BF16),
            pltpu.VMEM((rows, columns), BF16),
            pltpu.VMEM((columns, half), BF16),
            pltpu.VMEM((columns, half), BF16),
            pltpu.VMEM((2, rows, half), F32),
            pltpu.VMEM((2, 8, rows), F32),
            pltpu.VMEM((2, 8, rows), F32),
            pltpu.VMEM((MET, rows, half), BF16),
            pltpu.VMEM((MET, rows, half), BF16),
            pltpu.VMEM((MET, rows, rows), F32),
            pltpu.VMEM((MET, rows, rows), jnp.int16),
            pltpu.VMEM((MET, rows, rows), jnp.int16),
            pltpu.VMEM((MET, rows + EXTRA, rows), BF16),
            pltpu.VMEM((MET, rows + EXTRA, rows), BF16),
            pltpu.VMEM((rows, rows), F32),
            pltpu.VMEM((rows, rows), F32),
            pltpu.VMEM((GROUP, 2, rows, part), BF16),
            pltpu.VMEM((GROUP, 2, rows, part), BF16),
            pltpu.VMEM((2, 2, GROUP, rows, half // 2), BF16),
            pltpu.VMEM((2, 2, XS, part // XS, half // 2), F32),
            pltpu.VMEM((2, 2, XS, part // XS, half // 2), BF16),
            pltpu.VMEM((2, 2, XS - 1, part // XS, half // 2), BF16),
            pltpu.VMEM((2, 2, ZS, 16, half // 2), F32),
            pltpu.VMEM((2, 2, ZS, 16, half // 2), BF16),
            pltpu.VMEM((2, 2, ZS - 1, 16, half // 2), BF16),
            pltpu.SemaphoreType.DMA((4,)),
            pltpu.SemaphoreType.DMA((COPIES,)),
            pltpu.SemaphoreType.DMA((COPIES,)),
        ],
        compiler_params=pltpu.CompilerParams(
            collective_id=0, has_side_effects=True, vmem_limit_bytes=56 * 1024 * 1024
        ),
    )(
        picture_tower_summary, caption_tower_summary, picture_head_matrix, caption_head_matrix,
        matching_caption_row, affinity_scale, affinity_offset, jnp.asarray(column_order()),
    )
    loss, image_grad_w, text_grad_w = pl.pallas_call(
        results,
        out_shape=[
            jax.ShapeDtypeStruct((1, rows), F32),
            jax.ShapeDtypeStruct((12, half), F32),
            jax.ShapeDtypeStruct((12, half), F32),
        ],
        in_specs=[vmem] * 3,
        out_specs=[vmem] * 3,
    )(loss, image_grad_w, text_grad_w)
    return loss[0], image_grad_w, text_grad_w


def solution(mesh):
    return jax.shard_map(
        shards,
        mesh=mesh,
        in_specs=(
            P("dp", None),
            P("dp", None),
            P(None, "head"),
            P(None, "head"),
            P("dp", None),
            P(),
            P(),
        ),
        out_specs=(P("dp"), P("dp", "head"), P("dp", "head")),
        check_vma=False,
    )
```
